32 devices in a mesh: parts: 2 (over y), tensor: 4 (over z), dp: 4 (over x, core).
Axes of the slice: x: 2, y: 2, z: 4, core: 2. Of those that a mesh axis runs over, the one named last changes fastest.
Arguments:
- acts_in: bfloat16 [2, 16, 512, 8192], P(None, ('parts', 'dp'), None, 'tensor'), parts along dimension 1, may hold values from -6 to 6
- grads_out: bfloat16 [2, 16, 512, 8192], P(None, ('parts', 'dp'), None, 'tensor'), parts along dimension 1, may hold values from -6 to 6
- basis_in: bfloat16 [2, 8192, 64], P(None, 'tensor'), may hold values from -0.0625 to 0.0625
- basis_out: bfloat16 [2, 8192, 64], P(None, 'tensor'), may hold values from -0.0625 to 0.0625
- lengths: int32 [16], P(('parts', 'dp')), parts along dimension 0, may hold values from 64 to 512, as said below
- fisher_inv: bfloat16 [2, 4096, 4096], P(None, 'dp', 'tensor'), may hold values from -3 to 3
- queries: bfloat16 [2, 1024, 4096], P(None, 'tensor', 'dp'), may hold values from -0.75 to 0.75
Outputs:
- scores: float32 [16, 1024], P(('parts', 'dp'), 'tensor'), parts along dimension 0
The draws below stay inside these ranges and needn't reach their ends.
There are 2 independent parts, one for each index of `parts`. The reference program is written for one: setup_inputs(seed, part) draws one part's arguments, and reference() takes and returns one part's arrays. A program takes and returns all parts, laid end to end along the dimension named above; an argument that names none is the same for every part. Nothing has to cross between parts.
Inputs may be any that keep to these rules, and one draw needn't show every extreme that they name: `lengths`: positions at or beyond an example's length are padding; some example has all 512 tokens.
All inputs are finite; a program needn't handle non-finite values.
Results may differ from the reference program's by a relative error of at most 0.0003.
Values may be sent and summed in bfloat16 or wider, within the bound.
No kernel may reach another device: no remote copies, remote signals or barrier semaphores. Data moves between devices by JAX's collectives and lax.ppermute only.
A program may use at most 128 MiB of HBM per device.

```python
import math
import jax
import jax.numpy as jnp
from jax import lax

D = 8192
R = 64
K = 4096
LAYERS = 2
LEN = 512
EX = 8
NQ = 1024


def draw_lengths(key, part):
    key = jax.random.fold_in(key, 11)
    drawn_len = jax.random.randint(key, (EX,), LEN // 8, LEN + 1)
    chosen = jax.random.randint(jax.random.fold_in(key, 1), (), 0, EX)
    slots = lax.broadcasted_iota(jnp.int32, (EX,), 0)
    return jnp.where(slots == chosen, LEN, drawn_len).astype(jnp.int32)


def draw_fisher_inv(key, part):
    key = jax.random.fold_in(key, 23)
    first_key, second_key = jax.random.split(key)
    spread_part = jax.random.uniform(first_key, (LAYERS, K, K), jnp.float32, -1.0, 1.0) * (1.2 / math.sqrt(K))
    diagonal = jnp.exp(jax.random.uniform(second_key, (LAYERS, K), jnp.float32, math.log(0.5), math.log(2.0)))
    rows_idx = lax.broadcasted_iota(jnp.int32, (K, K), 0)
    cols_idx = lax.broadcasted_iota(jnp.int32, (K, K), 1)
    identity_mask = jnp.where(rows_idx == cols_idx, 1.0, 0.0).astype(jnp.float32)
    return (spread_part + identity_mask[None, :, :] * diagonal[:, :, None]).astype(jnp.bfloat16)


def block_scale(key, dims, cuts, least, largest):
    factor_of, own = 1.0, jax.random.fold_in(key, 6)
    for dim, blocks in cuts:
        draws = jnp.exp(jax.random.uniform(jax.random.fold_in(own, dim), (blocks,), jnp.float32, least / len(cuts), largest / len(cuts)))
        factor_of = factor_of * jnp.repeat(draws, dims[dim] // blocks).reshape([-1 if axis == dim else 1 for axis in range(len(dims))])
    return factor_of


def centred(own_key, dims, deviation, most, cuts=(), held_as=jnp.bfloat16):
    level = block_scale(own_key, dims, cuts, -0.22, 0.18) if cuts else 1.0
    drawn = jax.random.normal(own_key, dims, jnp.float32) * deviation * level
    return jnp.minimum(jnp.maximum(drawn, -most), most).astype(held_as)


def setup_inputs(seed: int = 0, part: int = 0) -> dict:
    splits = jax.random.split(jax.random.key(seed), 8)
    part_splits = jax.random.split(jax.random.fold_in(splits[7], part), 8)
    return {
        "acts_in": centred(part_splits[0], (LAYERS, EX, LEN, D), 1.0, 6.0, ((1, 4), (3, 4))),
        "grads_out": centred(part_splits[1], (LAYERS, EX, LEN, D), 1.0, 6.0, ((1, 4), (3, 4))),
        "basis_in": centred(splits[2], (LAYERS, D, R), D ** -0.5, 0.0625, ((1, 4),)),
        "basis_out": centred(splits[3], (LAYERS, D, R), D ** -0.5, 0.0625, ((1, 4),)),
        "lengths": draw_lengths(jax.random.fold_in(jax.random.fold_in(splits[7], part), 71), part),
        "fisher_inv": draw_fisher_inv(jax.random.fold_in(splits[7], 71), part),
        "queries": centred(splits[6], (LAYERS, NQ, K), 0.125, 0.75, ((1, 4), (2, 4))),
    }


def reference(acts_in, grads_out, basis_in, basis_out, lengths, fisher_inv, queries):
    scores = jnp.zeros((EX, NQ), jnp.float32)
    positions = lax.broadcasted_iota(jnp.int32, (LEN,), 0)
    for layer_idx in range(LAYERS):
        side_in = basis_in[layer_idx]
        side_out = basis_out[layer_idx]

        def per_example(inputs):
            acts, grads, count = inputs
            proj_in = jnp.dot(acts, side_in, preferred_element_type=jnp.float32)
            proj_out = jnp.dot(grads, side_out, preferred_element_type=jnp.float32)
            token_weight = jnp.where(positions < count, 1.0, 0.0).astype(jnp.float32) / count.astype(jnp.float32)
            outer_prod = jnp.dot((proj_out * token_weight[:, None]).T, proj_in, precision=lax.Precision.HIGHEST)
            return outer_prod.reshape(R * R)

        example_grads = lax.map(per_example, (acts_in[layer_idx], grads_out[layer_idx], lengths))
        mapped = jnp.dot(example_grads, fisher_inv[layer_idx].astype(jnp.float32), precision=lax.Precision.HIGHEST)
        scores = scores + jnp.dot(mapped, queries[layer_idx].astype(jnp.float32).T, precision=lax.Precision.HIGHEST)
    return scores
```

```python
import jax
import jax.numpy as jnp
from jax import lax
from jax.experimental import pallas as pl
from jax.experimental.pallas import tpu as pltpu
from jax.sharding import PartitionSpec as P

STEPS = 64.0
TOP = 32767.0
CHUNKS = 2
AHEAD = 2
VMEM = 24 * 1024 * 1024


def nn(a, b):
    return lax.dot_general(a, b, (((1,), (0,)), ((), ())), preferred_element_type=jnp.float32)


def nt(a, b):
    return lax.dot_general(a, b, (((1,), (1,)), ((), ())), preferred_element_type=jnp.float32)


def tn(a, b):
    return lax.dot_general(a, b, (((0,), (0,)), ((), ())), preferred_element_type=jnp.float32)


def thirds(x):
    first = x.astype(jnp.bfloat16).astype(jnp.float32)
    rest = x - first
    second = rest.astype(jnp.bfloat16).astype(jnp.float32)
    return jnp.concatenate([first, second, rest - second], axis=0).astype(jnp.bfloat16)


def add_thirds(x):
    rows = x.shape[0] // 3
    return x[:rows] + (x[rows : 2 * rows] + x[2 * rows :])


def project(flips, groups, acts, grads, basis_in, basis_out, *refs):
    outs, (a_buf, g_buf, in_buf, out_buf, scale_log, sems, basis_sems) = refs[: len(flips)], refs[len(flips) :]
    examples, tokens = acts.shape[1], acts.shape[2]
    here = lax.axis_index("tensor")
    layer = (here ^ flips[0]) // examples
    size = tokens // CHUNKS
    bases = (
        pltpu.make_async_copy(basis_out.at[layer], out_buf, basis_sems.at[0]),
        pltpu.make_async_copy(basis_in.at[layer], in_buf, basis_sems.at[1]),
    )
    copies = []
    for k, flip in enumerate(flips):
        example = (here ^ flip) % examples
        for c in range(CHUNKS):
            rows, at = pl.ds(c * size, size), k * CHUNKS + c
            copies.append(
                (
                    pltpu.make_async_copy(grads.at[layer, example, rows, :], g_buf.at[at], sems.at[0, at]),
                    pltpu.make_async_copy(acts.at[layer, example, rows, :], a_buf.at[at], sems.at[1, at]),
                )
            )
    for copy in bases:
        copy.start()
    for c in range(AHEAD):
        for copy in copies[c]:
            copy.start()
    for copy in bases:
        copy.wait()
    for k, out in enumerate(outs):
        for c in range(CHUNKS):
            rows, at = pl.ds(c * size, size), k * CHUNKS + c
            for copy in copies[at]:
                copy.wait()
            if at + AHEAD < len(copies):
                for copy in copies[at + AHEAD]:
                    copy.start()
            proj_out = nt(g_buf[at], out_buf[...])
            proj_in = nt(a_buf[at], in_buf[...])
            both = jnp.concatenate([proj_out, proj_in], axis=1)
            group = groups[k]
            if not group:
                out[rows, :] = both
                continue
            grouped = both.reshape(size // group, group, both.shape[1])
            most = jnp.maximum(jnp.max(jnp.abs(grouped), axis=1), 1e-30)
            log = jnp.ceil(jnp.log2(most) * STEPS)
            scale = jnp.exp2(log * (-1.0 / STEPS)) * TOP
            codes = jnp.round(grouped * scale[:, None, :])
            codes = jnp.minimum(jnp.maximum(codes, -TOP), TOP).reshape(both.shape)
            out[rows, :] = codes.astype(jnp.int32).astype(jnp.int16)
            scale_log[pl.ds(c * (size // group), size // group), :] = log
        if group:
            log = scale_log[pl.ds(0, tokens // group), :]
            out[pl.ds(tokens, tokens // group), :] = log.astype(jnp.int32).astype(jnp.int16)


def projector(flips, groups, acts, grads, basis_in, basis_out):
    tokens, width = acts.shape[2], acts.shape[3]
    both = 2 * basis_in.shape[1]

    def project_pairs(*refs):
        project(flips, groups, *refs)

    pieces = len(flips) * CHUNKS
    hbm = pl.BlockSpec(memory_space=pltpu.HBM)
    vmem = pl.BlockSpec(memory_space=pltpu.VMEM)
    return pl.pallas_call(
        project_pairs,
        out_shape=[
            jax.ShapeDtypeStruct((tokens + tokens // g, both), jnp.int16)
            if g
            else jax.ShapeDtypeStruct((tokens, both), jnp.float32)
            for g in groups
        ],
        in_specs=[hbm] * 4,
        out_specs=[vmem] * len(groups),
        scratch_shapes=[
            pltpu.VMEM((pieces, tokens // CHUNKS, width), acts.dtype),
            pltpu.VMEM((pieces, tokens // CHUNKS, width), grads.dtype),
            pltpu.VMEM(basis_in.shape[1:], basis_in.dtype),
            pltpu.VMEM(basis_out.shape[1:], basis_out.dtype),
            pltpu.VMEM((tokens // 16, both), jnp.float32),
            pltpu.SemaphoreType.DMA((2, pieces)),
            pltpu.SemaphoreType.DMA((2,)),
        ],
        compiler_params=pltpu.CompilerParams(vmem_limit_bytes=VMEM),
        cost_estimate=pl.CostEstimate(
            flops=2 * len(flips) * tokens * width * both,
            bytes_accessed=4 * len(flips) * tokens * width,
            transcendentals=0,
        ),
    )(*(pltpu.with_memory_space_constraint(x, pltpu.HBM) for x in (acts, grads, basis_in, basis_out)))


def outer(lengths, own, *refs):
    coded, out, grad = refs[:-2], refs[-2], refs[-1]
    tokens, both = own.shape
    half = both // 2
    example = lax.axis_index("tensor") % lengths.shape[0]
    count = lengths[example]
    total = own[...]
    for ref in coded:
        shared = ref.shape[0] - tokens
        log = ref[pl.ds(tokens, shared), :].astype(jnp.int32).astype(jnp.float32)
        scale = jnp.exp2(log * (1.0 / STEPS)) * (1.0 / TOP)
        codes = ref[pl.ds(0, tokens), :].astype(jnp.int32).astype(jnp.float32)
        codes = codes.reshape(shared, tokens // shared, both) * scale[:, None, :]
        total = total + codes.reshape(tokens, both)
    row = lax.broadcasted_iota(jnp.int32, (tokens, both), 0)
    lane = lax.broadcasted_iota(jnp.int32, (tokens, both), 1)
    kept = jnp.where(row < count, total, 0.0)
    weighted = jnp.where(lane < half, kept / count.astype(jnp.float32), kept)
    first = weighted.astype(jnp.bfloat16)
    rest = (weighted - first.astype(jnp.float32)).astype(jnp.bfloat16)
    product = tn(first, first) + (tn(first, rest) + tn(rest, first))
    grad[...] = product[:half, :]
    even = grad[pl.ds(0, half // 2, stride=2), :][:, half:]
    odd = grad[pl.ds(1, half // 2, stride=2), :][:, half:]
    blocks = jnp.concatenate([even, odd], axis=1)
    block_rows = blocks.shape[0] // 2
    for t in range(4):
        for x in range(2):
            out[t * 2 + x] = blocks[x * block_rows : (x + 1) * block_rows]


def through_fisher(grads, fisher, beside, out):
    layers, depth, width = fisher.shape
    lanes = grads.shape[2]
    rows = grads.shape[0] // layers
    cut = out.shape[2]
    halves = width // cut
    core = lax.axis_index("core")
    steps = depth // lanes
    for layer in range(layers):
        mapped = None
        for block, owner in ((fisher, core), (beside, 1 - core)):
            parts = [
                jnp.concatenate([grads[layer * rows + s, pl.ds(owner * steps + r, 1), :] for s in range(rows)], axis=0)
                for r in range(steps)
            ]
            term = nn(thirds(jnp.concatenate(parts, axis=1)), block[layer])
            mapped = term if mapped is None else mapped + term
        mapped = add_thirds(mapped)
        for x in range(2):
            for e in range(rows // 2):
                row = e * 2 + x
                for h in range(halves):
                    at = (layer * (rows // 2) + e) * halves + h
                    piece = mapped[row : row + 1, h * cut : (h + 1) * cut]
                    for t in range(4):
                        out[t * 2 + x, pl.ds(at, 1), :] = piece


def with_queries(mapped, *refs):
    queries, out = refs[:-1], refs[-1]
    layers = queries[0].shape[0]
    groups = len(queries)
    rows, cut = mapped.shape[1], mapped.shape[2]
    halves = queries[0].shape[2] // cut
    examples = rows // (layers * halves)
    here = lax.axis_index("x") * 2 + lax.axis_index("core")
    sums = [None] * (layers * halves)
    for k, block in enumerate(queries):
        column = here ^ k
        left = thirds(mapped[column * 2] + mapped[column * 2 + 1])
        for layer in range(layers):
            for h in range(halves):
                term = nt(left, block[layer, :, h * cut : (h + 1) * cut])
                at = layer * halves + h
                sums[at] = term if sums[at] is None else sums[at] + term
    result = [None] * examples
    for layer in range(layers):
        for h in range(halves):
            scores = add_thirds(sums[layer * halves + h])
            for e in range(examples):
                row = (layer * examples + e) * halves + h
                term = scores[row : row + 1]
                result[e] = term if result[e] is None else result[e] + term
    out[...] = jnp.concatenate(result, axis=0)


def swap(x, axis, flip):
    return lax.ppermute(x, axis, [(i, i ^ flip) for i in range(lax.axis_size(axis))])


def in_vmem(x):
    return pltpu.with_memory_space_constraint(x, pltpu.VMEM)


def small(acts_in, grads_out, basis_in, basis_out, lengths, fisher_inv, queries):
    vmem = pl.BlockSpec(memory_space=pltpu.VMEM)
    params = pltpu.CompilerParams(vmem_limit_bytes=VMEM)
    proj_width = basis_in.shape[2]
    operands = (acts_in, grads_out, jnp.swapaxes(basis_in, 1, 2), jnp.swapaxes(basis_out, 1, 2))

    far, middle = projector((3, 2), (16, 16), *operands)
    acts_in, grads_out, far, middle = lax.optimization_barrier((acts_in, grads_out, far, middle))
    far, middle = swap(far, "tensor", 3), swap(middle, "tensor", 2)
    near, own = projector((1, 0), (32, 0), acts_in, grads_out, *operands[2:])
    far, near, own, fisher_inv, queries = lax.optimization_barrier((far, near, own, fisher_inv, queries))
    near = swap(near, "tensor", 1)
    across = swap(queries, "x", 1)
    fisher_beside = swap(fisher_inv, "core", 1)
    beside = swap(queries, "core", 1)

    blocks = pl.pallas_call(
        outer,
        out_shape=jax.ShapeDtypeStruct((8, proj_width // 4, 2 * proj_width), jnp.float32),
        in_specs=[pl.BlockSpec(memory_space=pltpu.SMEM)] + [vmem] * 4,
        out_specs=vmem,
        scratch_shapes=[pltpu.VMEM((proj_width, 2 * proj_width), jnp.float32)],
        compiler_params=params,
    )(lengths, own, far, middle, near)
    blocks, beside, fisher_beside = lax.optimization_barrier((blocks, beside, fisher_beside))
    blocks = lax.all_to_all(blocks, ("tensor", "x"), 0, 0, tiled=True)

    mapped = pl.pallas_call(
        through_fisher,
        out_shape=jax.ShapeDtypeStruct((8, 8, fisher_inv.shape[2] // 2), jnp.float32),
        in_specs=[vmem] * 3,
        out_specs=vmem,
        compiler_params=params,
    )(blocks, in_vmem(fisher_inv), in_vmem(fisher_beside))
    across, mapped = lax.optimization_barrier((across, mapped))
    corner = swap(across, "core", 1)
    mapped = lax.all_to_all(mapped, ("tensor", "x"), 0, 0, tiled=True)

    return pl.pallas_call(
        with_queries,
        out_shape=jax.ShapeDtypeStruct((acts_in.shape[1], queries.shape[1]), jnp.float32),
        in_specs=[vmem] * 5,
        out_specs=vmem,
        compiler_params=params,
    )(mapped, queries, beside, across, corner)


def general(acts_in, grads_out, basis_in, basis_out, lengths, fisher_inv, queries):
    proj_width = basis_in.shape[2]
    layer_count = acts_in.shape[0]
    local_examples = acts_in.shape[1]
    proj_in = jnp.einsum("letd,ldr->letr", acts_in, basis_in, preferred_element_type=jnp.float32)
    proj_out = jnp.einsum(
        "letd,ldr->letr", grads_out, basis_out, preferred_element_type=jnp.float32
    )
    partial_proj = jnp.concatenate([proj_out, proj_in], axis=3)
    summed_proj = lax.psum(partial_proj, "tensor")
    share_len = summed_proj.shape[2]
    proj_out = summed_proj[..., :proj_width]
    proj_in = summed_proj[..., proj_width:]
    positions = lax.broadcasted_iota(jnp.int32, (share_len,), 0)
    token_weight = jnp.where(positions[None, :] < lengths[:, None], 1.0, 0.0).astype(jnp.float32)
    token_weight = token_weight / lengths[:, None].astype(jnp.float32)
    weighted = proj_out * token_weight[None, :, :, None]
    outer_prod = jnp.einsum("leta,letb->leab", weighted, proj_in, precision=lax.Precision.HIGHEST)
    example_grads = outer_prod.reshape(layer_count, local_examples, proj_width * proj_width)
    row_blocks = lax.all_to_all(example_grads, "dp", split_axis=2, concat_axis=1, tiled=True)
    gathered_queries = lax.all_gather(queries, "dp", axis=2, tiled=True)
    mapped = jnp.einsum(
        "lqj,lij->lqi",
        gathered_queries,
        lax.all_gather(fisher_inv, "tensor", axis=2, tiled=True),
        preferred_element_type=jnp.float32,
    )
    score_terms = jnp.einsum("lei,lqi->eq", row_blocks, mapped, precision=lax.Precision.HIGHEST)
    return lax.psum_scatter(score_terms, "dp", scatter_dimension=0, tiled=True)


def solution(mesh):
    dp = ("dp",)
    local = general
    if mesh.shape["tensor"] == 4 and mesh.shape["dp"] == 4:
        mesh = jax.sharding.Mesh(mesh.devices.reshape(-1, 4, 2, 2), ("parts", "tensor", "x", "core"))
        dp = ("x", "core")
        local = small
    in_specs = (
        P(None, ("parts", *dp), None, "tensor"),
        P(None, ("parts", *dp), None, "tensor"),
        P(None, "tensor", None),
        P(None, "tensor", None),
        P(("parts", *dp)),
        P(None, dp, "tensor"),
        P(None, "tensor", dp),
    )
    out_specs = P(("parts", *dp), "tensor")
    return jax.shard_map(local, mesh=mesh, in_specs=in_specs, out_specs=out_specs, check_vma=False)
```

```python
import jax
import jax.numpy as jnp
from jax import lax
from jax.experimental import pallas as pl
from jax.experimental.pallas import tpu as pltpu
from jax.sharding import PartitionSpec as P

STEPS = 64.0
TOP = 32767.0
CHUNKS = 2
AHEAD = 2
VMEM = 24 * 1024 * 1024


def nn(a, b):
    return lax.dot_general(a, b, (((1,), (0,)), ((), ())), preferred_element_type=jnp.float32)


def nt(a, b):
    return lax.dot_general(a, b, (((1,), (1,)), ((), ())), preferred_element_type=jnp.float32)


def tn(a, b):
    return lax.dot_general(a, b, (((0,), (0,)), ((), ())), preferred_element_type=jnp.float32)


def thirds(x):
    first = x.astype(jnp.bfloat16).astype(jnp.float32)
    rest = x - first
    second = rest.astype(jnp.bfloat16).astype(jnp.float32)
    return jnp.concatenate([first, second, rest - second], axis=0).astype(jnp.bfloat16)


def add_thirds(x):
    rows = x.shape[0] // 3
    return x[:rows] + (x[rows : 2 * rows] + x[2 * rows :])


def project(flips, groups, moves, acts, grads, basis_in, basis_out, *refs):
    *refs, a_buf, g_buf, in_buf, out_buf, scale_log, sems, basis_sems, move_sems = refs
    outs = refs[-len(flips) :]
    examples, tokens = acts.shape[1], acts.shape[2]
    here = lax.axis_index("tensor")
    layer = (here ^ flips[0]) // examples
    size = tokens // CHUNKS
    bases = (
        pltpu.make_async_copy(basis_out.at[layer], out_buf, basis_sems.at[0]),
        pltpu.make_async_copy(basis_in.at[layer], in_buf, basis_sems.at[1]),
    )
    copies = []
    for k, flip in enumerate(flips):
        example = (here ^ flip) % examples
        for c in range(CHUNKS):
            rows, at = pl.ds(c * size, size), k * CHUNKS + c
            copies.append(
                (
                    pltpu.make_async_copy(grads.at[layer, example, rows, :], g_buf.at[at], sems.at[0, at]),
                    pltpu.make_async_copy(acts.at[layer, example, rows, :], a_buf.at[at], sems.at[1, at]),
                )
            )
    moved = [
        pltpu.make_async_copy(source, target, move_sems.at[i])
        for i, (source, target) in enumerate(moves(*refs[: -len(flips)]))
    ]
    for copy in bases:
        copy.start()
    for c in range(AHEAD):
        for copy in copies[c]:
            copy.start()
    for copy in bases:
        copy.wait()
    for k, out in enumerate(outs):
        group = groups[k]
        for c in range(CHUNKS):
            rows, at = pl.ds(c * size, size), k * CHUNKS + c
            for copy in copies[at]:
                copy.wait()
            if at + AHEAD < len(copies):
                for copy in copies[at + AHEAD]:
                    copy.start()
            elif at + AHEAD == len(copies):
                for copy in moved:
                    copy.start()
            proj_out = nt(g_buf[at], out_buf[...])
            proj_in = nt(a_buf[at], in_buf[...])
            both = jnp.concatenate([proj_out, proj_in], axis=1)
            if not group:
                out[rows, :] = both
                continue
            grouped = both.reshape(size // group, group, both.shape[1])
            most = jnp.maximum(jnp.max(jnp.abs(grouped), axis=1), 1e-30)
            log = jnp.ceil(jnp.log2(most) * STEPS)
            scale = jnp.exp2(log * (-1.0 / STEPS)) * TOP
            codes = jnp.round(grouped * scale[:, None, :])
            codes = jnp.minimum(jnp.maximum(codes, -TOP), TOP).reshape(both.shape)
            out[rows, :] = codes.astype(jnp.int32).astype(jnp.int16)
            scale_log[pl.ds(c * (size // group), size // group), :] = log
        if group:
            log = scale_log[pl.ds(0, tokens // group), :]
            out[pl.ds(tokens, tokens // group), :] = log.astype(jnp.int32).astype(jnp.int16)
    for copy in moved:
        copy.wait()


def no_moves():
    return ()


def projector(flips, groups, acts, grads, basis_in, basis_out, sources=(), targets=(), moves=no_moves, count=1):
    tokens, width = acts.shape[2], acts.shape[3]
    both = 2 * basis_in.shape[1]
    pieces = len(flips) * CHUNKS
    operands = (acts, grads, basis_in, basis_out, *sources)
    hbm = pl.BlockSpec(memory_space=pltpu.HBM)
    vmem = pl.BlockSpec(memory_space=pltpu.VMEM)

    def project_pairs(*refs):
        project(flips, groups, moves, *refs)

    return pl.pallas_call(
        project_pairs,
        out_shape=[*targets]
        + [
            jax.ShapeDtypeStruct((tokens + tokens // g, both), jnp.int16)
            if g
            else jax.ShapeDtypeStruct((tokens, both), jnp.float32)
            for g in groups
        ],
        in_specs=[hbm] * len(operands),
        out_specs=[vmem] * (len(targets) + len(groups)),
        scratch_shapes=[
            pltpu.VMEM((pieces, tokens // CHUNKS, width), acts.dtype),
            pltpu.VMEM((pieces, tokens // CHUNKS, width), grads.dtype),
            pltpu.VMEM(basis_in.shape[1:], basis_in.dtype),
            pltpu.VMEM(basis_out.shape[1:], basis_out.dtype),
            pltpu.VMEM((tokens // 16, both), jnp.float32),
            pltpu.SemaphoreType.DMA((2, pieces)),
            pltpu.SemaphoreType.DMA((2,)),
            pltpu.SemaphoreType.DMA((count,)),
        ],
        compiler_params=pltpu.CompilerParams(vmem_limit_bytes=VMEM),
        cost_estimate=pl.CostEstimate(
            flops=2 * len(flips) * tokens * width * both,
            bytes_accessed=4 * len(flips) * tokens * width,
            transcendentals=0,
        ),
    )(*(pltpu.with_memory_space_constraint(x, pltpu.HBM) for x in operands))


def blocks_together(fisher, queries, both):
    for layer in range(fisher.shape[0]):
        depth, rows = fisher.shape[1], queries.shape[1]
        yield fisher.at[layer], both.at[layer, pl.ds(0, depth), :]
        yield queries.at[layer], both.at[layer, pl.ds(depth, rows), :]


def decode(ref, tokens):
    shared = ref.shape[0] - tokens
    both = ref.shape[1]
    log = ref[pl.ds(tokens, shared), :].astype(jnp.int32).astype(jnp.float32)
    scale = jnp.exp2(log * (1.0 / STEPS)) * (1.0 / TOP)
    codes = ref[pl.ds(0, tokens), :].astype(jnp.int32).astype(jnp.float32)
    return (codes.reshape(shared, tokens // shared, both) * scale[:, None, :]).reshape(tokens, both)


def add_up(own, first, second, out):
    tokens = own.shape[0]
    out[...] = own[...] + decode(first, tokens) + decode(second, tokens)


def outer(lengths, most, last, out, grad):
    tokens, both = most.shape
    half = both // 2
    example = lax.axis_index("tensor") % lengths.shape[0]
    count = lengths[example]
    total = most[...] + decode(last, tokens)
    row = lax.broadcasted_iota(jnp.int32, (tokens, both), 0)
    lane = lax.broadcasted_iota(jnp.int32, (tokens, both), 1)
    kept = jnp.where(row < count, total, 0.0)
    weighted = jnp.where(lane < half, kept / count.astype(jnp.float32), kept)
    first = weighted.astype(jnp.bfloat16)
    rest = (weighted - first.astype(jnp.float32)).astype(jnp.bfloat16)
    product = tn(first, first) + (tn(first, rest) + tn(rest, first))
    grad[...] = product[:half, :]
    even = grad[pl.ds(0, half // 2, stride=2), :][:, half:]
    odd = grad[pl.ds(1, half // 2, stride=2), :][:, half:]
    blocks = jnp.concatenate([even, odd], axis=1)
    block_rows = blocks.shape[0] // 2
    for t in range(4):
        for x in range(2):
            out[t * 2 + x] = blocks[x * block_rows : (x + 1) * block_rows]


def through_fisher(grads, fisher, beside, out):
    layers, _, width = fisher.shape
    lanes = grads.shape[2]
    rows = grads.shape[0] // layers
    depth = grads.shape[1] * lanes // 2
    cut = out.shape[2]
    halves = width // cut
    core = lax.axis_index("core")
    steps = depth // lanes
    for layer in range(layers):
        mapped = None
        for block, owner in ((fisher, core), (beside, 1 - core)):
            parts = [
                jnp.concatenate([grads[layer * rows + s, pl.ds(owner * steps + r, 1), :] for s in range(rows)], axis=0)
                for r in range(steps)
            ]
            term = nn(thirds(jnp.concatenate(parts, axis=1)), block[layer, pl.ds(0, depth), :])
            mapped = term if mapped is None else mapped + term
        mapped = add_thirds(mapped)
        for x in range(2):
            for e in range(rows // 2):
                row = e * 2 + x
                for h in range(halves):
                    at = (layer * (rows // 2) + e) * halves + h
                    piece = mapped[row : row + 1, h * cut : (h + 1) * cut]
                    for t in range(4):
                        out[t * 2 + x, pl.ds(at, 1), :] = piece


def with_queries(mapped, own, beside, across, corner, out):
    layers, cut = own.shape[0], mapped.shape[2]
    halves = own.shape[2] // cut
    count = out.shape[1]
    examples = mapped.shape[1] // (layers * halves)
    here = lax.axis_index("x") * 2 + lax.axis_index("core")
    sums = [None] * (layers * halves)
    for k, block in enumerate((own, beside, across, corner)):
        left = thirds(mapped[(here ^ k) * 2] + mapped[(here ^ k) * 2 + 1])
        rows = pl.ds(block.shape[1] - count, count)
        for layer in range(layers):
            for h in range(halves):
                term = nt(left, block[layer, rows, h * cut : (h + 1) * cut])
                at = layer * halves + h
                sums[at] = term if sums[at] is None else sums[at] + term
    result = [None] * examples
    for layer in range(layers):
        for h in range(halves):
            scores = add_thirds(sums[layer * halves + h])
            for e in range(examples):
                row = (layer * examples + e) * halves + h
                term = scores[row : row + 1]
                result[e] = term if result[e] is None else result[e] + term
    out[...] = jnp.concatenate(result, axis=0)


def swap(x, axis, flip):
    return lax.ppermute(x, axis, [(i, i ^ flip) for i in range(lax.axis_size(axis))])


def in_vmem(x):
    return pltpu.with_memory_space_constraint(x, pltpu.VMEM)


def small(acts_in, grads_out, basis_in, basis_out, lengths, fisher_inv, queries):
    vmem = pl.BlockSpec(memory_space=pltpu.VMEM)
    params = pltpu.CompilerParams(vmem_limit_bytes=VMEM)
    proj_width = basis_in.shape[2]
    operands = (acts_in, grads_out, jnp.swapaxes(basis_in, 1, 2), jnp.swapaxes(basis_out, 1, 2))

    far, middle = projector((3, 2), (16, 16), *operands)
    acts_in, grads_out, fisher_inv, queries, far, middle = lax.optimization_barrier(
        (acts_in, grads_out, fisher_inv, queries, far, middle)
    )
    far, middle = swap(far, "tensor", 3), swap(middle, "tensor", 2)
    across = swap(queries, "x", 1)
    near, here = projector((1, 0), (32, 0), acts_in, grads_out, *operands[2:])
    near = swap(near, "tensor", 1)
    fisher_beside = swap(fisher_inv, "core", 1)

    most = pl.pallas_call(
        add_up,
        out_shape=jax.ShapeDtypeStruct(here.shape, jnp.float32),
        in_specs=[vmem] * 3,
        out_specs=vmem,
        compiler_params=params,
        cost_estimate=pl.CostEstimate(flops=0, bytes_accessed=1 << 21, transcendentals=0),
    )(here, far, middle)

    blocks = pl.pallas_call(
        outer,
        out_shape=jax.ShapeDtypeStruct((8, proj_width // 4, 2 * proj_width), jnp.float32),
        in_specs=[pl.BlockSpec(memory_space=pltpu.SMEM)] + [vmem] * 2,
        out_specs=vmem,
        scratch_shapes=[pltpu.VMEM((proj_width, 2 * proj_width), jnp.float32)],
        compiler_params=params,
    )(lengths, most, near)
    blocks, fisher_beside = lax.optimization_barrier((blocks, fisher_beside))
    blocks = lax.all_to_all(blocks, ("tensor", "x"), 0, 0, tiled=True)

    mapped = pl.pallas_call(
        through_fisher,
        out_shape=jax.ShapeDtypeStruct((8, 8, fisher_inv.shape[2] // 2), jnp.float32),
        in_specs=[vmem] * 3,
        out_specs=vmem,
        compiler_params=params,
    )(blocks, in_vmem(fisher_inv), in_vmem(fisher_beside))
    across, queries, mapped = lax.optimization_barrier((across, queries, mapped))
    corner, beside = swap(across, "core", 1), swap(queries, "core", 1)
    mapped = lax.all_to_all(mapped, ("tensor", "x"), 0, 0, tiled=True)

    return pl.pallas_call(
        with_queries,
        out_shape=jax.ShapeDtypeStruct((acts_in.shape[1], queries.shape[1]), jnp.float32),
        in_specs=[vmem] * 5,
        out_specs=vmem,
        compiler_params=params,
    )(mapped, queries, beside, across, corner)


def general(acts_in, grads_out, basis_in, basis_out, lengths, fisher_inv, queries):
    proj_width = basis_in.shape[2]
    layer_count = acts_in.shape[0]
    local_examples = acts_in.shape[1]
    proj_in = jnp.einsum("letd,ldr->letr", acts_in, basis_in, preferred_element_type=jnp.float32)
    proj_out = jnp.einsum(
        "letd,ldr->letr", grads_out, basis_out, preferred_element_type=jnp.float32
    )
    partial_proj = jnp.concatenate([proj_out, proj_in], axis=3)
    summed_proj = lax.psum(partial_proj, "tensor")
    share_len = summed_proj.shape[2]
    proj_out = summed_proj[..., :proj_width]
    proj_in = summed_proj[..., proj_width:]
    positions = lax.broadcasted_iota(jnp.int32, (share_len,), 0)
    token_weight = jnp.where(positions[None, :] < lengths[:, None], 1.0, 0.0).astype(jnp.float32)
    token_weight = token_weight / lengths[:, None].astype(jnp.float32)
    weighted = proj_out * token_weight[None, :, :, None]
    outer_prod = jnp.einsum("leta,letb->leab", weighted, proj_in, precision=lax.Precision.HIGHEST)
    example_grads = outer_prod.reshape(layer_count, local_examples, proj_width * proj_width)
    row_blocks = lax.all_to_all(example_grads, "dp", split_axis=2, concat_axis=1, tiled=True)
    gathered_queries = lax.all_gather(queries, "dp", axis=2, tiled=True)
    mapped = jnp.einsum(
        "lqj,lij->lqi",
        gathered_queries,
        lax.all_gather(fisher_inv, "tensor", axis=2, tiled=True),
        preferred_element_type=jnp.float32,
    )
    score_terms = jnp.einsum("lei,lqi->eq", row_blocks, mapped, precision=lax.Precision.HIGHEST)
    return lax.psum_scatter(score_terms, "dp", scatter_dimension=0, tiled=True)


def solution(mesh):
    dp = ("dp",)
    local = general
    if (mesh.shape["parts"], mesh.shape["tensor"], mesh.shape["dp"]) == (2, 4, 4):
        mesh = jax.sharding.Mesh(mesh.devices.reshape(2, 4, 2, 2), ("parts", "tensor", "x", "core"))
        dp = ("x", "core")
        local = small
    in_specs = (
        P(None, ("parts", *dp), None, "tensor"),
        P(None, ("parts", *dp), None, "tensor"),
        P(None, "tensor", None),
        P(None, "tensor", None),
        P(("parts", *dp)),
        P(None, dp, "tensor"),
        P(None, "tensor", dp),
    )
    out_specs = P(("parts", *dp), "tensor")
    return jax.shard_map(local, mesh=mesh, in_specs=in_specs, out_specs=out_specs, check_vma=False)
```

```python
import jax
import jax.numpy as jnp
from jax import lax
from jax.experimental import pallas as pl
from jax.experimental.pallas import tpu as pltpu
from jax.sharding import PartitionSpec as P

STEPS = 64.0
TOP = 32767.0
PIECES_TWO = ((128, 384), (256, 256))
PIECES_ONE = ((128, 384),)
AHEAD = 2
VMEM = 24 * 1024 * 1024


def nn(a, b):
    return lax.dot_general(a, b, (((1,), (0,)), ((), ())), preferred_element_type=jnp.float32)


def nt(a, b):
    return lax.dot_general(a, b, (((1,), (1,)), ((), ())), preferred_element_type=jnp.float32)


def tn(a, b):
    return lax.dot_general(a, b, (((0,), (0,)), ((), ())), preferred_element_type=jnp.float32)


def thirds(x):
    first = x.astype(jnp.bfloat16).astype(jnp.float32)
    rest = x - first
    second = rest.astype(jnp.bfloat16).astype(jnp.float32)
    return jnp.concatenate([first, second, rest - second], axis=0).astype(jnp.bfloat16)


def add_thirds(x):
    rows = x.shape[0] // 3
    return x[:rows] + (x[rows : 2 * rows] + x[2 * rows :])


def project(flips, groups, pieces, turn, acts, grads, basis_in, basis_out, *refs):
    *refs, a_buf, g_buf, in_buf, out_buf, scale_log, sems, basis_sems = refs
    queries = turned = turn_buf = None
    if turn:
        *refs, turn_buf = refs
        queries, turned, *refs = refs
    outs = refs
    examples, tokens = acts.shape[1], acts.shape[2]
    here = lax.axis_index("tensor")
    layer = (here ^ flips[0]) // examples
    first = [
        pltpu.make_async_copy(basis_out.at[layer], out_buf, basis_sems.at[0]),
        pltpu.make_async_copy(basis_in.at[layer], in_buf, basis_sems.at[1]),
    ]
    if turn:
        first.append(pltpu.make_async_copy(queries, turn_buf, basis_sems.at[2]))
    copies, spans = [], []
    for k, flip in enumerate(flips):
        example = (here ^ flip) % examples
        begin = 0
        for size in pieces[k]:
            rows, at = pl.ds(begin, size), len(copies)
            spans.append((k, begin, size))
            copies.append(
                (
                    pltpu.make_async_copy(grads.at[layer, example, rows, :], g_buf.at[k, rows, :], sems.at[0, at]),
                    pltpu.make_async_copy(acts.at[layer, example, rows, :], a_buf.at[k, rows, :], sems.at[1, at]),
                )
            )
            begin += size
    for copy in first:
        copy.start()
    for c in range(AHEAD):
        for copy in copies[c]:
            copy.start()
    for copy in first:
        copy.wait()
    if turn:
        for q in range(turned.shape[0]):
            turned[q] = turn_buf[q].T
    for at, (k, begin, size) in enumerate(spans):
        group, out, rows = groups[k], outs[k], pl.ds(begin, size)
        for copy in copies[at]:
            copy.wait()
        if at + AHEAD < len(copies):
            for copy in copies[at + AHEAD]:
                copy.start()
        proj_out = nt(g_buf[k, rows, :], out_buf[...])
        proj_in = nt(a_buf[k, rows, :], in_buf[...])
        both = jnp.concatenate([proj_out, proj_in], axis=1)
        if not group:
            out[rows, :] = both
            continue
        grouped = both.reshape(size // group, group, both.shape[1])
        most = jnp.maximum(jnp.max(jnp.abs(grouped), axis=1), 1e-30)
        log = jnp.ceil(jnp.log2(most) * STEPS)
        scale = jnp.exp2(log * (-1.0 / STEPS)) * TOP
        codes = jnp.round(grouped * scale[:, None, :])
        codes = jnp.minimum(jnp.maximum(codes, -TOP), TOP).reshape(both.shape)
        out[rows, :] = codes.astype(jnp.int32).astype(jnp.int16)
        scale_log[pl.ds(begin // group, size // group), :] = log
        if begin + size == tokens:
            log = scale_log[pl.ds(0, tokens // group), :]
            out[pl.ds(tokens, tokens // group), :] = log.astype(jnp.int32).astype(jnp.int16)


def projector(flips, groups, pieces, acts, grads, basis_in, basis_out, queries=None):
    tokens, width = acts.shape[2], acts.shape[3]
    both = 2 * basis_in.shape[1]
    steps = sum(len(p) for p in pieces)
    operands, turned, turn_buf = [acts, grads, basis_in, basis_out], [], []
    if queries is not None:
        layers, count, depth = queries.shape
        operands.append(queries)
        turned = [jax.ShapeDtypeStruct((layers, depth, count), queries.dtype)]
        turn_buf = [pltpu.VMEM(queries.shape, queries.dtype)]
    hbm = pl.BlockSpec(memory_space=pltpu.HBM)
    vmem = pl.BlockSpec(memory_space=pltpu.VMEM)

    def project_pairs(*refs):
        project(flips, groups, pieces, queries is not None, *refs)

    return pl.pallas_call(
        project_pairs,
        out_shape=turned
        + [
            jax.ShapeDtypeStruct((tokens + tokens // g, both), jnp.int16)
            if g
            else jax.ShapeDtypeStruct((tokens, both), jnp.float32)
            for g in groups
        ],
        in_specs=[hbm] * len(operands),
        out_specs=[vmem] * (len(turned) + len(groups)),
        scratch_shapes=turn_buf
        + [
            pltpu.VMEM((len(flips), tokens, width), acts.dtype),
            pltpu.VMEM((len(flips), tokens, width), grads.dtype),
            pltpu.VMEM(basis_in.shape[1:], basis_in.dtype),
            pltpu.VMEM(basis_out.shape[1:], basis_out.dtype),
            pltpu.VMEM((tokens // 16, both), jnp.float32),
            pltpu.SemaphoreType.DMA((2, steps)),
            pltpu.SemaphoreType.DMA((3,)),
        ],
        compiler_params=pltpu.CompilerParams(vmem_limit_bytes=VMEM),
        cost_estimate=pl.CostEstimate(
            flops=2 * len(flips) * tokens * width * both,
            bytes_accessed=4 * len(flips) * tokens * width,
            transcendentals=0,
        ),
    )(*(pltpu.with_memory_space_constraint(x, pltpu.HBM) for x in operands))


def decode(ref, tokens):
    shared = ref.shape[0] - tokens
    both = ref.shape[1]
    log = ref[pl.ds(tokens, shared), :].astype(jnp.int32).astype(jnp.float32)
    scale = jnp.exp2(log * (1.0 / STEPS)) * (1.0 / TOP)
    codes = ref[pl.ds(0, tokens), :].astype(jnp.int32).astype(jnp.float32)
    return (codes.reshape(shared, tokens // shared, both) * scale[:, None, :]).reshape(tokens, both)


def add_up(own, first, second, out):
    tokens = own.shape[0]
    out[...] = own[...] + decode(first, tokens) + decode(second, tokens)


def outer(lengths, most, last, out, grad):
    tokens, both = most.shape
    half = both // 2
    example = lax.axis_index("tensor") % lengths.shape[0]
    count = lengths[example]
    total = most[...] + decode(last, tokens)
    row = lax.broadcasted_iota(jnp.int32, (tokens, both), 0)
    lane = lax.broadcasted_iota(jnp.int32, (1, both), 1)
    weight = jnp.where(lane < half, 1.0 / jnp.full((1, both), count, jnp.int32).astype(jnp.float32), 1.0)
    weighted = jnp.where(row < count, total * weight, 0.0)
    first = weighted.astype(jnp.bfloat16)
    rest = (weighted - first.astype(jnp.float32)).astype(jnp.bfloat16)
    wide = tn(first, jnp.concatenate([first, rest], axis=1))
    product = wide[:, :both] + (wide[:, both:] + tn(rest, first))
    grad[...] = product[:half, :]
    even = grad[pl.ds(0, half // 2, stride=2), :][:, half:]
    odd = grad[pl.ds(1, half // 2, stride=2), :][:, half:]
    blocks = jnp.concatenate([even, odd], axis=1)
    block_rows = blocks.shape[0] // 2
    for t in range(4):
        for x in range(2):
            out[t * 2 + x] = blocks[x * block_rows : (x + 1) * block_rows]


def through_fisher(grads, fisher, beside, out):
    layers, _, width = fisher.shape
    lanes = grads.shape[2]
    rows = grads.shape[0] // layers
    depth = grads.shape[1] * lanes // 2
    cut = out.shape[2]
    halves = width // cut
    core = lax.axis_index("core")
    steps = depth // lanes
    order = [e * 2 + x for x in range(2) for e in range(rows // 2)]
    every = []
    for layer in range(layers):
        mapped = None
        for block, owner in ((fisher, core), (beside, 1 - core)):
            parts = [
                jnp.concatenate([grads[layer * rows + s, pl.ds(owner * steps + r, 1), :] for s in order], axis=0)
                for r in range(steps)
            ]
            term = nn(thirds(jnp.concatenate(parts, axis=1)), block[layer, pl.ds(0, depth), :])
            mapped = term if mapped is None else mapped + term
        every.append(add_thirds(mapped))
    for x in range(2):
        own = jnp.concatenate([mapped[x * rows // 2 : (x + 1) * rows // 2] for mapped in every], axis=0)
        mapped = jnp.concatenate([own[:, h * cut : (h + 1) * cut] for h in range(halves)], axis=0)
        for t in range(4):
            out[t * 2 + x] = mapped


def with_queries(mapped, own, beside, across, corner, out):
    layers, depth, count = own.shape
    halves = depth // mapped.shape[2]
    rows = mapped.shape[1] // halves
    here = lax.axis_index("x") * 2 + lax.axis_index("core")
    sums = [None] * layers
    for k, block in enumerate((own, beside, across, corner)):
        both = mapped[(here ^ k) * 2] + mapped[(here ^ k) * 2 + 1]
        left = thirds(jnp.concatenate([both[h * rows : (h + 1) * rows] for h in range(halves)], axis=1))
        for layer in range(layers):
            term = nn(left, block[layer])
            sums[layer] = term if sums[layer] is None else sums[layer] + term
    examples = rows // layers
    result = None
    for layer in range(layers):
        scores = add_thirds(sums[layer])[layer * examples : (layer + 1) * examples]
        result = scores if result is None else result + scores
    out[...] = result


def swap(x, axis, flip):
    return lax.ppermute(x, axis, [(i, i ^ flip) for i in range(lax.axis_size(axis))])


def in_vmem(x):
    return pltpu.with_memory_space_constraint(x, pltpu.VMEM)


def small(acts_in, grads_out, basis_in, basis_out, lengths, fisher_inv, queries):
    vmem = pl.BlockSpec(memory_space=pltpu.VMEM)
    params = pltpu.CompilerParams(vmem_limit_bytes=VMEM)
    proj_width = basis_in.shape[2]
    operands = (acts_in, grads_out, jnp.swapaxes(basis_in, 1, 2), jnp.swapaxes(basis_out, 1, 2))

    queries, far, middle = projector((3, 2), (32, 32), PIECES_TWO, *operands, queries)
    acts_in, grads_out, queries, far, middle = lax.optimization_barrier((acts_in, grads_out, queries, far, middle))
    far, middle = swap(far, "tensor", 3), swap(middle, "tensor", 2)
    across = swap(queries, "x", 1)
    (near,) = projector((1,), (32,), PIECES_ONE, acts_in, grads_out, *operands[2:])
    (here,) = projector((0,), (0,), PIECES_ONE, acts_in, grads_out, *operands[2:])
    near = swap(near, "tensor", 1)
    fisher_beside = swap(fisher_inv, "core", 1)

    most = pl.pallas_call(
        add_up,
        out_shape=jax.ShapeDtypeStruct(here.shape, jnp.float32),
        in_specs=[vmem] * 3,
        out_specs=vmem,
        compiler_params=params,
        cost_estimate=pl.CostEstimate(flops=0, bytes_accessed=1 << 21, transcendentals=0),
    )(here, far, middle)

    blocks = pl.pallas_call(
        outer,
        out_shape=jax.ShapeDtypeStruct((8, proj_width // 4, 2 * proj_width), jnp.float32),
        in_specs=[pl.BlockSpec(memory_space=pltpu.SMEM)] + [vmem] * 2,
        out_specs=vmem,
        scratch_shapes=[pltpu.VMEM((proj_width, 2 * proj_width), jnp.float32)],
        compiler_params=params,
    )(lengths, most, near)
    blocks, fisher_beside = lax.optimization_barrier((blocks, fisher_beside))
    blocks = lax.all_to_all(blocks, ("tensor", "x"), 0, 0, tiled=True)

    mapped = pl.pallas_call(
        through_fisher,
        out_shape=jax.ShapeDtypeStruct((8, 8, fisher_inv.shape[2] // 2), jnp.float32),
        in_specs=[vmem] * 3,
        out_specs=vmem,
        compiler_params=params,
    )(blocks, in_vmem(fisher_inv), in_vmem(fisher_beside))
    across, queries, mapped = lax.optimization_barrier((across, queries, mapped))
    corner, beside = swap(across, "core", 1), swap(queries, "core", 1)
    mapped = lax.all_to_all(mapped, ("tensor", "x"), 0, 0, tiled=True)

    return pl.pallas_call(
        with_queries,
        out_shape=jax.ShapeDtypeStruct((acts_in.shape[1], queries.shape[2]), jnp.float32),
        in_specs=[vmem] * 5,
        out_specs=vmem,
        compiler_params=params,
    )(mapped, queries, beside, across, corner)


def general(acts_in, grads_out, basis_in, basis_out, lengths, fisher_inv, queries):
    proj_width = basis_in.shape[2]
    layer_count = acts_in.shape[0]
    local_examples = acts_in.shape[1]
    proj_in = jnp.einsum("letd,ldr->letr", acts_in, basis_in, preferred_element_type=jnp.float32)
    proj_out = jnp.einsum(
        "letd,ldr->letr", grads_out, basis_out, preferred_element_type=jnp.float32
    )
    partial_proj = jnp.concatenate([proj_out, proj_in], axis=3)
    summed_proj = lax.psum(partial_proj, "tensor")
    share_len = summed_proj.shape[2]
    proj_out = summed_proj[..., :proj_width]
    proj_in = summed_proj[..., proj_width:]
    positions = lax.broadcasted_iota(jnp.int32, (share_len,), 0)
    token_weight = jnp.where(positions[None, :] < lengths[:, None], 1.0, 0.0).astype(jnp.float32)
    token_weight = token_weight / lengths[:, None].astype(jnp.float32)
    weighted = proj_out * token_weight[None, :, :, None]
    outer_prod = jnp.einsum("leta,letb->leab", weighted, proj_in, precision=lax.Precision.HIGHEST)
    example_grads = outer_prod.reshape(layer_count, local_examples, proj_width * proj_width)
    row_blocks = lax.all_to_all(example_grads, "dp", split_axis=2, concat_axis=1, tiled=True)
    gathered_queries = lax.all_gather(queries, "dp", axis=2, tiled=True)
    mapped = jnp.einsum(
        "lqj,lij->lqi",
        gathered_queries,
        lax.all_gather(fisher_inv, "tensor", axis=2, tiled=True),
        preferred_element_type=jnp.float32,
    )
    score_terms = jnp.einsum("lei,lqi->eq", row_blocks, mapped, precision=lax.Precision.HIGHEST)
    return lax.psum_scatter(score_terms, "dp", scatter_dimension=0, tiled=True)


def solution(mesh):
    dp = ("dp",)
    local = general
    if (mesh.shape["parts"], mesh.shape["tensor"], mesh.shape["dp"]) == (2, 4, 4):
        mesh = jax.sharding.Mesh(mesh.devices.reshape(2, 4, 2, 2), ("parts", "tensor", "x", "core"))
        dp = ("x", "core")
        local = small
    in_specs = (
        P(None, ("parts", *dp), None, "tensor"),
        P(None, ("parts", *dp), None, "tensor"),
        P(None, "tensor", None),
        P(None, "tensor", None),
        P(("parts", *dp)),
        P(None, dp, "tensor"),
        P(None, "tensor", dp),
    )
    out_specs = P(("parts", *dp), "tensor")
    return jax.shard_map(local, mesh=mesh, in_specs=in_specs, out_specs=out_specs, check_vma=False)
```

```python
import jax
import jax.numpy as jnp
from jax import lax
from jax.experimental import pallas as pl
from jax.experimental.pallas import tpu as pltpu
from jax.sharding import PartitionSpec as P

STEPS = 64.0
TOP = 32767.0
PIECES_TWO = ((128, 384), (256, 256))
PIECES_ONE = ((128, 384),)
AHEAD = 2
VMEM = 24 * 1024 * 1024


def nn(a, b):
    return lax.dot_general(a, b, (((1,), (0,)), ((), ())), preferred_element_type=jnp.float32)


def nt(a, b):
    return lax.dot_general(a, b, (((1,), (1,)), ((), ())), preferred_element_type=jnp.float32)


def tn(a, b):
    return lax.dot_general(a, b, (((0,), (0,)), ((), ())), preferred_element_type=jnp.float32)


def thirds(x):
    first = x.astype(jnp.bfloat16).astype(jnp.float32)
    rest = x - first
    second = rest.astype(jnp.bfloat16).astype(jnp.float32)
    return jnp.concatenate([first, second, rest - second], axis=0).astype(jnp.bfloat16)


def add_thirds(x):
    rows = x.shape[0] // 3
    return x[:rows] + (x[rows : 2 * rows] + x[2 * rows :])


def project(flips, groups, pieces, turn, acts, grads, basis_in, basis_out, *refs):
    *refs, a_buf, g_buf, in_buf, out_buf, scale_log, sems, basis_sems = refs
    queries = turned = turn_buf = None
    if turn:
        *refs, turn_buf = refs
        queries, turned, *refs = refs
    outs = refs
    examples, tokens = acts.shape[1], acts.shape[2]
    here = lax.axis_index("tensor")
    layer = (here ^ flips[0]) // examples
    first = [
        pltpu.make_async_copy(basis_out.at[layer], out_buf, basis_sems.at[0]),
        pltpu.make_async_copy(basis_in.at[layer], in_buf, basis_sems.at[1]),
    ]
    if turn:
        first.append(pltpu.make_async_copy(queries, turn_buf, basis_sems.at[2]))
    copies, spans = [], []
    for k, flip in enumerate(flips):
        example = (here ^ flip) % examples
        begin = 0
        for size in pieces[k]:
            rows, at = pl.ds(begin, size), len(copies)
            spans.append((k, begin, size))
            copies.append(
                (
                    pltpu.make_async_copy(grads.at[layer, example, rows, :], g_buf.at[k, rows, :], sems.at[0, at]),
                    pltpu.make_async_copy(acts.at[layer, example, rows, :], a_buf.at[k, rows, :], sems.at[1, at]),
                )
            )
            begin += size
    for copy in first:
        copy.start()
    for c in range(AHEAD):
        for copy in copies[c]:
            copy.start()
    for copy in first:
        copy.wait()
    if turn:
        for q in range(turned.shape[0]):
            turned[q] = turn_buf[q].T
    for at, (k, begin, size) in enumerate(spans):
        group, out, rows = groups[k], outs[k], pl.ds(begin, size)
        for copy in copies[at]:
            copy.wait()
        if at + AHEAD < len(copies):
            for copy in copies[at + AHEAD]:
                copy.start()
        proj_out = nt(g_buf[k, rows, :], out_buf[...])
        proj_in = nt(a_buf[k, rows, :], in_buf[...])
        both = jnp.concatenate([proj_out, proj_in], axis=1)
        if not group:
            out[rows, :] = both
            continue
        grouped = both.reshape(size // group, group, both.shape[1])
        most = jnp.maximum(jnp.max(jnp.abs(grouped), axis=1), 1e-30)
        log = jnp.ceil(jnp.log2(most) * STEPS)
        scale = jnp.exp2(log * (-1.0 / STEPS)) * TOP
        codes = jnp.round(grouped * scale[:, None, :])
        codes = jnp.minimum(jnp.maximum(codes, -TOP), TOP).reshape(both.shape)
        out[rows, :] = codes.astype(jnp.int32).astype(jnp.int16)
        scale_log[pl.ds(begin // group, size // group), :] = log
        if begin + size == tokens:
            log = scale_log[pl.ds(0, tokens // group), :]
            out[pl.ds(tokens, tokens // group), :] = log.astype(jnp.int32).astype(jnp.int16)


def projector(flips, groups, pieces, acts, grads, basis_in, basis_out, queries=None):
    tokens, width = acts.shape[2], acts.shape[3]
    both = 2 * basis_in.shape[1]
    steps = sum(len(p) for p in pieces)
    operands, turned, turn_buf = [acts, grads, basis_in, basis_out], [], []
    if queries is not None:
        layers, count, depth = queries.shape
        operands.append(queries)
        turned = [jax.ShapeDtypeStruct((layers, depth, count), queries.dtype)]
        turn_buf = [pltpu.VMEM(queries.shape, queries.dtype)]
    hbm = pl.BlockSpec(memory_space=pltpu.HBM)
    vmem = pl.BlockSpec(memory_space=pltpu.VMEM)

    def project_pairs(*refs):
        project(flips, groups, pieces, queries is not None, *refs)

    return pl.pallas_call(
        project_pairs,
        out_shape=turned
        + [
            jax.ShapeDtypeStruct((tokens + tokens // g, both), jnp.int16)
            if g
            else jax.ShapeDtypeStruct((tokens, both), jnp.float32)
            for g in groups
        ],
        in_specs=[hbm] * len(operands),
        out_specs=[vmem] * (len(turned) + len(groups)),
        scratch_shapes=turn_buf
        + [
            pltpu.VMEM((len(flips), tokens, width), acts.dtype),
            pltpu.VMEM((len(flips), tokens, width), grads.dtype),
            pltpu.VMEM(basis_in.shape[1:], basis_in.dtype),
            pltpu.VMEM(basis_out.shape[1:], basis_out.dtype),
            pltpu.VMEM((tokens // 16, both), jnp.float32),
            pltpu.SemaphoreType.DMA((2, steps)),
            pltpu.SemaphoreType.DMA((3,)),
        ],
        compiler_params=pltpu.CompilerParams(vmem_limit_bytes=VMEM),
        cost_estimate=pl.CostEstimate(
            flops=2 * len(flips) * tokens * width * both,
            bytes_accessed=4 * len(flips) * tokens * width,
            transcendentals=0,
        ),
    )(*(pltpu.with_memory_space_constraint(x, pltpu.HBM) for x in operands))


def decode(ref, tokens):
    shared = ref.shape[0] - tokens
    both = ref.shape[1]
    log = ref[pl.ds(tokens, shared), :].astype(jnp.int32).astype(jnp.float32)
    scale = jnp.exp2(log * (1.0 / STEPS)) * (1.0 / TOP)
    codes = ref[pl.ds(0, tokens), :].astype(jnp.int32).astype(jnp.float32)
    return (codes.reshape(shared, tokens // shared, both) * scale[:, None, :]).reshape(tokens, both)


def add_up(own, first, second, out):
    tokens = own.shape[0]
    out[...] = own[...] + decode(first, tokens) + decode(second, tokens)


def outer(lengths, most, last, out, grad):
    tokens, both = most.shape
    half = both // 2
    example = lax.axis_index("tensor") % lengths.shape[0]
    count = lengths[example]
    total = most[...] + decode(last, tokens)
    row = lax.broadcasted_iota(jnp.int32, (tokens, both), 0)
    lane = lax.broadcasted_iota(jnp.int32, (1, both), 1)
    weight = jnp.where(lane < half, 1.0 / jnp.full((1, both), count, jnp.int32).astype(jnp.float32), 1.0)
    weighted = jnp.where(row < count, total * weight, 0.0)
    first = weighted.astype(jnp.bfloat16)
    rest = (weighted - first.astype(jnp.float32)).astype(jnp.bfloat16)
    wide = tn(first, jnp.concatenate([first, rest], axis=1))
    product = wide[:, :both] + (wide[:, both:] + tn(rest, first))
    grad[...] = product[:half, :]
    even = grad[pl.ds(0, half // 2, stride=2), :][:, half:]
    odd = grad[pl.ds(1, half // 2, stride=2), :][:, half:]
    blocks = jnp.concatenate([even, odd], axis=1)
    block_rows = blocks.shape[0] // 2
    for t in range(4):
        for x in range(2):
            out[t * 2 + x] = blocks[x * block_rows : (x + 1) * block_rows]


def through_fisher(grads, fisher, beside, out):
    layers, _, width = fisher.shape
    lanes = grads.shape[2]
    rows = grads.shape[0] // layers
    depth = grads.shape[1] * lanes // 2
    cut = out.shape[2]
    halves = width // cut
    core = lax.axis_index("core")
    steps = depth // lanes
    order = [e * 2 + x for x in range(2) for e in range(rows // 2)]
    every = []
    for layer in range(layers):
        mapped = None
        for block, owner in ((fisher, core), (beside, 1 - core)):
            parts = [
                jnp.concatenate([grads[layer * rows + s, pl.ds(owner * steps + r, 1), :] for s in order], axis=0)
                for r in range(steps)
            ]
            term = nn(thirds(jnp.concatenate(parts, axis=1)), block[layer, pl.ds(0, depth), :])
            mapped = term if mapped is None else mapped + term
        every.append(add_thirds(mapped))
    for x in range(2):
        own = jnp.concatenate([mapped[x * rows // 2 : (x + 1) * rows // 2] for mapped in every], axis=0)
        mapped = jnp.concatenate([own[:, h * cut : (h + 1) * cut] for h in range(halves)], axis=0)
        for t in range(4):
            out[t * 2 + x] = mapped


def with_queries(mapped, own, beside, across, corner, out):
    layers, depth, count = own.shape
    halves = depth // mapped.shape[2]
    rows = mapped.shape[1] // halves
    here = lax.axis_index("x") * 2 + lax.axis_index("core")
    sums = [None] * layers
    for k, block in enumerate((own, beside, across, corner)):
        both = mapped[(here ^ k) * 2] + mapped[(here ^ k) * 2 + 1]
        left = thirds(jnp.concatenate([both[h * rows : (h + 1) * rows] for h in range(halves)], axis=1))
        for layer in range(layers):
            term = nn(left, block[layer]) if k < 2 else nt(left, block[layer])
            sums[layer] = term if sums[layer] is None else sums[layer] + term
    examples = rows // layers
    result = None
    for layer in range(layers):
        scores = add_thirds(sums[layer])[layer * examples : (layer + 1) * examples]
        result = scores if result is None else result + scores
    out[...] = result


def swap(x, axis, flip):
    return lax.ppermute(x, axis, [(i, i ^ flip) for i in range(lax.axis_size(axis))])


def in_vmem(x):
    return pltpu.with_memory_space_constraint(x, pltpu.VMEM)


def small(acts_in, grads_out, basis_in, basis_out, lengths, fisher_inv, queries):
    vmem = pl.BlockSpec(memory_space=pltpu.VMEM)
    params = pltpu.CompilerParams(vmem_limit_bytes=VMEM)
    proj_width = basis_in.shape[2]
    operands = (acts_in, grads_out, jnp.swapaxes(basis_in, 1, 2), jnp.swapaxes(basis_out, 1, 2))

    across = swap(queries, "x", 1)
    queries, far, middle = projector((3, 2), (32, 32), PIECES_TWO, *operands, queries)
    acts_in, grads_out, far, middle = lax.optimization_barrier((acts_in, grads_out, far, middle))
    far, middle = swap(far, "tensor", 3), swap(middle, "tensor", 2)
    (near,) = projector((1,), (32,), PIECES_ONE, acts_in, grads_out, *operands[2:])
    (here,) = projector((0,), (0,), PIECES_ONE, acts_in, grads_out, *operands[2:])
    near = swap(near, "tensor", 1)
    fisher_beside = swap(fisher_inv, "core", 1)

    most = pl.pallas_call(
        add_up,
        out_shape=jax.ShapeDtypeStruct(here.shape, jnp.float32),
        in_specs=[vmem] * 3,
        out_specs=vmem,
        compiler_params=params,
        cost_estimate=pl.CostEstimate(flops=0, bytes_accessed=1 << 21, transcendentals=0),
    )(here, far, middle)

    blocks = pl.pallas_call(
        outer,
        out_shape=jax.ShapeDtypeStruct((8, proj_width // 4, 2 * proj_width), jnp.float32),
        in_specs=[pl.BlockSpec(memory_space=pltpu.SMEM)] + [vmem] * 2,
        out_specs=vmem,
        scratch_shapes=[pltpu.VMEM((proj_width, 2 * proj_width), jnp.float32)],
        compiler_params=params,
    )(lengths, most, near)
    blocks, fisher_beside = lax.optimization_barrier((blocks, fisher_beside))
    blocks = lax.all_to_all(blocks, ("tensor", "x"), 0, 0, tiled=True)

    mapped = pl.pallas_call(
        through_fisher,
        out_shape=jax.ShapeDtypeStruct((8, 8, fisher_inv.shape[2] // 2), jnp.float32),
        in_specs=[vmem] * 3,
        out_specs=vmem,
        compiler_params=params,
    )(blocks, in_vmem(fisher_inv), in_vmem(fisher_beside))
    across, queries, mapped = lax.optimization_barrier((across, queries, mapped))
    corner, beside = swap(across, "core", 1), swap(queries, "core", 1)
    mapped = lax.all_to_all(mapped, ("tensor", "x"), 0, 0, tiled=True)

    return pl.pallas_call(
        with_queries,
        out_shape=jax.ShapeDtypeStruct((acts_in.shape[1], queries.shape[2]), jnp.float32),
        in_specs=[vmem] * 5,
        out_specs=vmem,
        compiler_params=params,
    )(mapped, queries, beside, across, corner)


def general(acts_in, grads_out, basis_in, basis_out, lengths, fisher_inv, queries):
    proj_width = basis_in.shape[2]
    layer_count = acts_in.shape[0]
    local_examples = acts_in.shape[1]
    proj_in = jnp.einsum("letd,ldr->letr", acts_in, basis_in, preferred_element_type=jnp.float32)
    proj_out = jnp.einsum(
        "letd,ldr->letr", grads_out, basis_out, preferred_element_type=jnp.float32
    )
    partial_proj = jnp.concatenate([proj_out, proj_in], axis=3)
    summed_proj = lax.psum(partial_proj, "tensor")
    share_len = summed_proj.shape[2]
    proj_out = summed_proj[..., :proj_width]
    proj_in = summed_proj[..., proj_width:]
    positions = lax.broadcasted_iota(jnp.int32, (share_len,), 0)
    token_weight = jnp.where(positions[None, :] < lengths[:, None], 1.0, 0.0).astype(jnp.float32)
    token_weight = token_weight / lengths[:, None].astype(jnp.float32)
    weighted = proj_out * token_weight[None, :, :, None]
    outer_prod = jnp.einsum("leta,letb->leab", weighted, proj_in, precision=lax.Precision.HIGHEST)
    example_grads = outer_prod.reshape(layer_count, local_examples, proj_width * proj_width)
    row_blocks = lax.all_to_all(example_grads, "dp", split_axis=2, concat_axis=1, tiled=True)
    gathered_queries = lax.all_gather(queries, "dp", axis=2, tiled=True)
    mapped = jnp.einsum(
        "lqj,lij->lqi",
        gathered_queries,
        lax.all_gather(fisher_inv, "tensor", axis=2, tiled=True),
        preferred_element_type=jnp.float32,
    )
    score_terms = jnp.einsum("lei,lqi->eq", row_blocks, mapped, precision=lax.Precision.HIGHEST)
    return lax.psum_scatter(score_terms, "dp", scatter_dimension=0, tiled=True)


def solution(mesh):
    dp = ("dp",)
    local = general
    if (mesh.shape["parts"], mesh.shape["tensor"], mesh.shape["dp"]) == (2, 4, 4):
        mesh = jax.sharding.Mesh(mesh.devices.reshape(2, 4, 2, 2), ("parts", "tensor", "x", "core"))
        dp = ("x", "core")
        local = small
    in_specs = (
        P(None, ("parts", *dp), None, "tensor"),
        P(None, ("parts", *dp), None, "tensor"),
        P(None, "tensor", None),
        P(None, "tensor", None),
        P(("parts", *dp)),
        P(None, dp, "tensor"),
        P(None, "tensor", dp),
    )
    out_specs = P(("parts", *dp), "tensor")
    return jax.shard_map(local, mesh=mesh, in_specs=in_specs, out_specs=out_specs, check_vma=False)
```

```python
import jax
import jax.numpy as jnp
from jax import lax
from jax.experimental import pallas as pl
from jax.experimental.pallas import tpu as pltpu
from jax.sharding import PartitionSpec as P

STEPS = 64.0
TOP = 32767.0
PIECES_TWO = ((128, 384), (256, 256))
PIECES_ONE = ((128, 384),)
AHEAD = 2
VMEM = 24 * 1024 * 1024


def nn(a, b):
    return lax.dot_general(a, b, (((1,), (0,)), ((), ())), preferred_element_type=jnp.float32)


def nt(a, b):
    return lax.dot_general(a, b, (((1,), (1,)), ((), ())), preferred_element_type=jnp.float32)


def tn(a, b):
    return lax.dot_general(a, b, (((0,), (0,)), ((), ())), preferred_element_type=jnp.float32)


def thirds(x):
    first = x.astype(jnp.bfloat16).astype(jnp.float32)
    rest = x - first
    second = rest.astype(jnp.bfloat16).astype(jnp.float32)
    return jnp.concatenate([first, second, rest - second], axis=0).astype(jnp.bfloat16)


def add_thirds(x):
    rows = x.shape[0] // 3
    return x[:rows] + (x[rows : 2 * rows] + x[2 * rows :])


def project(flips, groups, pieces, turn, acts, grads, basis_in, basis_out, *refs):
    *refs, a_buf, g_buf, in_buf, out_buf, scale_log, sems, basis_sems = refs
    queries = beside = turned = turned_beside = turn_buf = None
    if turn:
        *refs, turn_buf = refs
        queries, beside, turned, turned_beside, *refs = refs
    outs = refs
    examples, tokens = acts.shape[1], acts.shape[2]
    here = lax.axis_index("tensor")
    layer = (here ^ flips[0]) // examples
    first = [
        pltpu.make_async_copy(basis_out.at[layer], out_buf, basis_sems.at[0]),
        pltpu.make_async_copy(basis_in.at[layer], in_buf, basis_sems.at[1]),
    ]
    if turn:
        first.append(pltpu.make_async_copy(queries, turn_buf, basis_sems.at[2]))
    copies, spans = [], []
    for k, flip in enumerate(flips):
        example = (here ^ flip) % examples
        begin = 0
        for size in pieces[k]:
            rows, at = pl.ds(begin, size), len(copies)
            spans.append((k, begin, size))
            copies.append(
                (
                    pltpu.make_async_copy(grads.at[layer, example, rows, :], g_buf.at[k, rows, :], sems.at[0, at]),
                    pltpu.make_async_copy(acts.at[layer, example, rows, :], a_buf.at[k, rows, :], sems.at[1, at]),
                )
            )
            begin += size
    for copy in first:
        copy.start()
    for c in range(AHEAD):
        for copy in copies[c]:
            copy.start()
    for copy in first:
        copy.wait()
    if turn:
        for i in range(turned.shape[0]):
            turned[i] = turn_buf[i].T
            turned_beside[i] = beside[i].T
    for at, (k, begin, size) in enumerate(spans):
        group, out, rows = groups[k], outs[k], pl.ds(begin, size)
        for copy in copies[at]:
            copy.wait()
        if at + AHEAD < len(copies):
            for copy in copies[at + AHEAD]:
                copy.start()
        proj_out = nt(g_buf[k, rows, :], out_buf[...])
        proj_in = nt(a_buf[k, rows, :], in_buf[...])
        both = jnp.concatenate([proj_out, proj_in], axis=1)
        if not group:
            out[rows, :] = both
            continue
        grouped = both.reshape(size // group, group, both.shape[1])
        most = jnp.maximum(jnp.max(jnp.abs(grouped), axis=1), 1e-30)
        log = jnp.ceil(jnp.log2(most) * STEPS)
        scale = jnp.exp2(log * (-1.0 / STEPS)) * TOP
        codes = jnp.round(grouped * scale[:, None, :])
        codes = jnp.minimum(jnp.maximum(codes, -TOP), TOP).reshape(both.shape)
        out[rows, :] = codes.astype(jnp.int32).astype(jnp.int16)
        scale_log[pl.ds(begin // group, size // group), :] = log
        if begin + size == tokens:
            log = scale_log[pl.ds(0, tokens // group), :]
            out[pl.ds(tokens, tokens // group), :] = log.astype(jnp.int32).astype(jnp.int16)


def projector(flips, groups, pieces, acts, grads, basis_in, basis_out, queries=None, beside=None):
    tokens, width = acts.shape[2], acts.shape[3]
    both = 2 * basis_in.shape[1]
    steps = sum(len(p) for p in pieces)
    operands, inside, turned, turn_buf = [acts, grads, basis_in, basis_out], [], [], []
    if queries is not None:
        operands.append(queries)
        inside.append(beside)
        layers, count, depth = queries.shape
        turned = [jax.ShapeDtypeStruct((layers, depth, count), queries.dtype)] * 2
        turn_buf = [pltpu.VMEM(queries.shape, queries.dtype)]
    hbm = pl.BlockSpec(memory_space=pltpu.HBM)
    vmem = pl.BlockSpec(memory_space=pltpu.VMEM)

    def project_pairs(*refs):
        project(flips, groups, pieces, queries is not None, *refs)

    return pl.pallas_call(
        project_pairs,
        out_shape=turned
        + [
            jax.ShapeDtypeStruct((tokens + tokens // g, both), jnp.int16)
            if g
            else jax.ShapeDtypeStruct((tokens, both), jnp.float32)
            for g in groups
        ],
        in_specs=[hbm] * len(operands) + [vmem] * len(inside),
        out_specs=[vmem] * (len(turned) + len(groups)),
        scratch_shapes=turn_buf
        + [
            pltpu.VMEM((len(flips), tokens, width), acts.dtype),
            pltpu.VMEM((len(flips), tokens, width), grads.dtype),
            pltpu.VMEM(basis_in.shape[1:], basis_in.dtype),
            pltpu.VMEM(basis_out.shape[1:], basis_out.dtype),
            pltpu.VMEM((tokens // 16, both), jnp.float32),
            pltpu.SemaphoreType.DMA((2, steps)),
            pltpu.SemaphoreType.DMA((3,)),
        ],
        compiler_params=pltpu.CompilerParams(vmem_limit_bytes=VMEM),
        cost_estimate=pl.CostEstimate(
            flops=2 * len(flips) * tokens * width * both,
            bytes_accessed=4 * len(flips) * tokens * width,
            transcendentals=0,
        ),
    )(*(pltpu.with_memory_space_constraint(x, pltpu.HBM) for x in operands), *inside)


def decode(ref, tokens):
    shared = ref.shape[0] - tokens
    both = ref.shape[1]
    log = ref[pl.ds(tokens, shared), :].astype(jnp.int32).astype(jnp.float32)
    scale = jnp.exp2(log * (1.0 / STEPS)) * (1.0 / TOP)
    codes = ref[pl.ds(0, tokens), :].astype(jnp.int32).astype(jnp.float32)
    return (codes.reshape(shared, tokens // shared, both) * scale[:, None, :]).reshape(tokens, both)


def add_up(own, first, second, out):
    tokens = own.shape[0]
    out[...] = own[...] + decode(first, tokens) + decode(second, tokens)


def outer(lengths, most, last, out, grad):
    tokens, both = most.shape
    half = both // 2
    example = lax.axis_index("tensor") % lengths.shape[0]
    count = lengths[example]
    total = most[...] + decode(last, tokens)
    row = lax.broadcasted_iota(jnp.int32, (tokens, both), 0)
    lane = lax.broadcasted_iota(jnp.int32, (1, both), 1)
    weight = jnp.where(lane < half, 1.0 / jnp.full((1, both), count, jnp.int32).astype(jnp.float32), 1.0)
    weighted = jnp.where(row < count, total * weight, 0.0)
    first = weighted.astype(jnp.bfloat16)
    rest = (weighted - first.astype(jnp.float32)).astype(jnp.bfloat16)
    wide = tn(first, jnp.concatenate([first, rest], axis=1))
    product = wide[:, :both] + (wide[:, both:] + tn(rest, first))
    grad[...] = product[:half, :]
    even = grad[pl.ds(0, half // 2, stride=2), :][:, half:]
    odd = grad[pl.ds(1, half // 2, stride=2), :][:, half:]
    blocks = jnp.concatenate([even, odd], axis=1)
    block_rows = blocks.shape[0] // 2
    for t in range(4):
        for x in range(2):
            out[t * 2 + x] = blocks[x * block_rows : (x + 1) * block_rows]


def through_fisher(grads, fisher, beside, out):
    layers, _, width = fisher.shape
    lanes = grads.shape[2]
    rows = grads.shape[0] // layers
    depth = grads.shape[1] * lanes // 2
    cut = out.shape[2]
    halves = width // cut
    core = lax.axis_index("core")
    steps = depth // lanes
    order = [e * 2 + x for x in range(2) for e in range(rows // 2)]
    every = []
    for layer in range(layers):
        mapped = None
        for block, owner in ((fisher, core), (beside, 1 - core)):
            parts = [
                jnp.concatenate([grads[layer * rows + s, pl.ds(owner * steps + r, 1), :] for s in order], axis=0)
                for r in range(steps)
            ]
            term = nn(thirds(jnp.concatenate(parts, axis=1)), block[layer, pl.ds(0, depth), :])
            mapped = term if mapped is None else mapped + term
        every.append(add_thirds(mapped))
    for x in range(2):
        own = jnp.concatenate([mapped[x * rows // 2 : (x + 1) * rows // 2] for mapped in every], axis=0)
        mapped = jnp.concatenate([own[:, h * cut : (h + 1) * cut] for h in range(halves)], axis=0)
        for t in range(4):
            out[t * 2 + x] = mapped


def with_queries(mapped, own, beside, across, corner, out):
    layers, depth, count = own.shape
    halves = depth // mapped.shape[2]
    rows = mapped.shape[1] // halves
    here = lax.axis_index("x") * 2 + lax.axis_index("core")
    sums = [None] * layers
    for k, block in enumerate((own, beside, across, corner)):
        both = mapped[(here ^ k) * 2] + mapped[(here ^ k) * 2 + 1]
        left = thirds(jnp.concatenate([both[h * rows : (h + 1) * rows] for h in range(halves)], axis=1))
        for layer in range(layers):
            term = nn(left, block[layer]) if k < 2 else nt(left, block[layer])
            sums[layer] = term if sums[layer] is None else sums[layer] + term
    examples = rows // layers
    result = None
    for layer in range(layers):
        scores = add_thirds(sums[layer])[layer * examples : (layer + 1) * examples]
        result = scores if result is None else result + scores
    out[...] = result


def swap(x, axis, flip):
    return lax.ppermute(x, axis, [(i, i ^ flip) for i in range(lax.axis_size(axis))])


def in_vmem(x):
    return pltpu.with_memory_space_constraint(x, pltpu.VMEM)


def small(acts_in, grads_out, basis_in, basis_out, lengths, fisher_inv, queries):
    vmem = pl.BlockSpec(memory_space=pltpu.VMEM)
    params = pltpu.CompilerParams(vmem_limit_bytes=VMEM)
    proj_width = basis_in.shape[2]
    operands = (acts_in, grads_out, jnp.swapaxes(basis_in, 1, 2), jnp.swapaxes(basis_out, 1, 2))

    across, beside = swap(queries, "x", 1), swap(queries, "core", 1)
    far, middle = projector((3, 2), (32, 32), PIECES_TWO, *operands)
    acts_in, grads_out, far, middle = lax.optimization_barrier((acts_in, grads_out, far, middle))
    far, middle = swap(far, "tensor", 3), swap(middle, "tensor", 2)
    (near,) = projector((1,), (32,), PIECES_ONE, acts_in, grads_out, *operands[2:])
    queries, beside, here = projector((0,), (0,), PIECES_ONE, acts_in, grads_out, *operands[2:], queries, beside)
    near = swap(near, "tensor", 1)
    fisher_beside = swap(fisher_inv, "core", 1)

    most = pl.pallas_call(
        add_up,
        out_shape=jax.ShapeDtypeStruct(here.shape, jnp.float32),
        in_specs=[vmem] * 3,
        out_specs=vmem,
        compiler_params=params,
        cost_estimate=pl.CostEstimate(flops=0, bytes_accessed=1 << 21, transcendentals=0),
    )(here, far, middle)

    blocks = pl.pallas_call(
        outer,
        out_shape=jax.ShapeDtypeStruct((8, proj_width // 4, 2 * proj_width), jnp.float32),
        in_specs=[pl.BlockSpec(memory_space=pltpu.SMEM)] + [vmem] * 2,
        out_specs=vmem,
        scratch_shapes=[pltpu.VMEM((proj_width, 2 * proj_width), jnp.float32)],
        compiler_params=params,
    )(lengths, most, near)
    blocks, fisher_beside = lax.optimization_barrier((blocks, fisher_beside))
    blocks = lax.all_to_all(blocks, ("tensor", "x"), 0, 0, tiled=True)

    mapped = pl.pallas_call(
        through_fisher,
        out_shape=jax.ShapeDtypeStruct((8, 8, fisher_inv.shape[2] // 2), jnp.float32),
        in_specs=[vmem] * 3,
        out_specs=vmem,
        compiler_params=params,
    )(blocks, in_vmem(fisher_inv), in_vmem(fisher_beside))
    across, mapped = lax.optimization_barrier((across, mapped))
    corner = swap(across, "core", 1)
    mapped = lax.all_to_all(mapped, ("tensor", "x"), 0, 0, tiled=True)

    return pl.pallas_call(
        with_queries,
        out_shape=jax.ShapeDtypeStruct((acts_in.shape[1], queries.shape[2]), jnp.float32),
        in_specs=[vmem] * 5,
        out_specs=vmem,
        compiler_params=params,
    )(mapped, queries, beside, across, corner)


def general(acts_in, grads_out, basis_in, basis_out, lengths, fisher_inv, queries):
    proj_width = basis_in.shape[2]
    layer_count = acts_in.shape[0]
    local_examples = acts_in.shape[1]
    proj_in = jnp.einsum("letd,ldr->letr", acts_in, basis_in, preferred_element_type=jnp.float32)
    proj_out = jnp.einsum(
        "letd,ldr->letr", grads_out, basis_out, preferred_element_type=jnp.float32
    )
    partial_proj = jnp.concatenate([proj_out, proj_in], axis=3)
    summed_proj = lax.psum(partial_proj, "tensor")
    share_len = summed_proj.shape[2]
    proj_out = summed_proj[..., :proj_width]
    proj_in = summed_proj[..., proj_width:]
    positions = lax.broadcasted_iota(jnp.int32, (share_len,), 0)
    token_weight = jnp.where(positions[None, :] < lengths[:, None], 1.0, 0.0).astype(jnp.float32)
    token_weight = token_weight / lengths[:, None].astype(jnp.float32)
    weighted = proj_out * token_weight[None, :, :, None]
    outer_prod = jnp.einsum("leta,letb->leab", weighted, proj_in, precision=lax.Precision.HIGHEST)
    example_grads = outer_prod.reshape(layer_count, local_examples, proj_width * proj_width)
    row_blocks = lax.all_to_all(example_grads, "dp", split_axis=2, concat_axis=1, tiled=True)
    gathered_queries = lax.all_gather(queries, "dp", axis=2, tiled=True)
    mapped = jnp.einsum(
        "lqj,lij->lqi",
        gathered_queries,
        lax.all_gather(fisher_inv, "tensor", axis=2, tiled=True),
        preferred_element_type=jnp.float32,
    )
    score_terms = jnp.einsum("lei,lqi->eq", row_blocks, mapped, precision=lax.Precision.HIGHEST)
    return lax.psum_scatter(score_terms, "dp", scatter_dimension=0, tiled=True)


def solution(mesh):
    dp = ("dp",)
    local = general
    if (mesh.shape["parts"], mesh.shape["tensor"], mesh.shape["dp"]) == (2, 4, 4):
        mesh = jax.sharding.Mesh(mesh.devices.reshape(2, 4, 2, 2), ("parts", "tensor", "x", "core"))
        dp = ("x", "core")
        local = small
    in_specs = (
        P(None, ("parts", *dp), None, "tensor"),
        P(None, ("parts", *dp), None, "tensor"),
        P(None, "tensor", None),
        P(None, "tensor", None),
        P(("parts", *dp)),
        P(None, dp, "tensor"),
        P(None, "tensor", dp),
    )
    out_specs = P(("parts", *dp), "tensor")
    return jax.shard_map(local, mesh=mesh, in_specs=in_specs, out_specs=out_specs, check_vma=False)
```

```python
import jax
import jax.numpy as jnp
from jax import lax
from jax.experimental import pallas as pl
from jax.experimental.pallas import tpu as pltpu
from jax.sharding import PartitionSpec as P

STEPS = 64.0
TOP = 32767.0
PIECES_TWO = ((128, 384), (256, 256))
PIECES_ONE = ((128, 384),)
AHEAD = 2
VMEM = 24 * 1024 * 1024


def nn(a, b):
    return lax.dot_general(a, b, (((1,), (0,)), ((), ())), preferred_element_type=jnp.float32)


def nt(a, b):
    return lax.dot_general(a, b, (((1,), (1,)), ((), ())), preferred_element_type=jnp.float32)


def tn(a, b):
    return lax.dot_general(a, b, (((0,), (0,)), ((), ())), preferred_element_type=jnp.float32)


def thirds(x):
    first = x.astype(jnp.bfloat16).astype(jnp.float32)
    rest = x - first
    second = rest.astype(jnp.bfloat16).astype(jnp.float32)
    return jnp.concatenate([first, second, rest - second], axis=0).astype(jnp.bfloat16)


def add_thirds(x):
    rows = x.shape[0] // 3
    return x[:rows] + (x[rows : 2 * rows] + x[2 * rows :])


def project(flips, groups, pieces, turn, acts, grads, basis_in, basis_out, *refs):
    *refs, a_buf, g_buf, in_buf, out_buf, scale_log, sems, basis_sems = refs
    queries = beside = turned = turned_beside = turn_buf = None
    if turn:
        *refs, turn_buf = refs
        queries, beside, turned, turned_beside, *refs = refs
    outs = refs
    examples, tokens = acts.shape[1], acts.shape[2]
    here = lax.axis_index("tensor")
    layers = [(here ^ flip) // examples for flip in flips]
    first = []
    for k, layer in enumerate(layers):
        first.append(pltpu.make_async_copy(basis_out.at[layer], out_buf.at[k], basis_sems.at[0, k]))
        first.append(pltpu.make_async_copy(basis_in.at[layer], in_buf.at[k], basis_sems.at[1, k]))
    if turn:
        first.append(pltpu.make_async_copy(queries, turn_buf, basis_sems.at[2, 0]))
    copies, spans = [], []
    for k, flip in enumerate(flips):
        example = (here ^ flip) % examples
        begin = 0
        for size in pieces[k]:
            rows, at = pl.ds(begin, size), len(copies)
            spans.append((k, begin, size))
            copies.append(
                (
                    pltpu.make_async_copy(grads.at[layers[k], example, rows, :], g_buf.at[k, rows, :], sems.at[0, at]),
                    pltpu.make_async_copy(acts.at[layers[k], example, rows, :], a_buf.at[k, rows, :], sems.at[1, at]),
                )
            )
            begin += size
    for copy in first:
        copy.start()
    for c in range(AHEAD):
        for copy in copies[c]:
            copy.start()
    for copy in first:
        copy.wait()
    if turn:
        for i in range(turned.shape[0]):
            turned[i] = turn_buf[i].T
            turned_beside[i] = beside[i].T
    for at, (k, begin, size) in enumerate(spans):
        group, out, rows = groups[k], outs[k], pl.ds(begin, size)
        for copy in copies[at]:
            copy.wait()
        if at + AHEAD < len(copies):
            for copy in copies[at + AHEAD]:
                copy.start()
        proj_out = nt(g_buf[k, rows, :], out_buf[k])
        proj_in = nt(a_buf[k, rows, :], in_buf[k])
        both = jnp.concatenate([proj_out, proj_in], axis=1)
        if not group:
            out[rows, :] = both
            continue
        grouped = both.reshape(size // group, group, both.shape[1])
        most = jnp.maximum(jnp.max(jnp.abs(grouped), axis=1), 1e-30)
        log = jnp.ceil(jnp.log2(most) * STEPS)
        scale = jnp.exp2(log * (-1.0 / STEPS)) * TOP
        codes = jnp.round(grouped * scale[:, None, :])
        codes = jnp.minimum(jnp.maximum(codes, -TOP), TOP).reshape(both.shape)
        out[rows, :] = codes.astype(jnp.int32).astype(jnp.int16)
        scale_log[pl.ds(begin // group, size // group), :] = log
        if begin + size == tokens:
            log = scale_log[pl.ds(0, tokens // group), :]
            out[pl.ds(tokens, tokens // group), :] = log.astype(jnp.int32).astype(jnp.int16)


def projector(flips, groups, pieces, acts, grads, basis_in, basis_out, queries=None, beside=None):
    tokens, width = acts.shape[2], acts.shape[3]
    both = 2 * basis_in.shape[1]
    steps = sum(len(p) for p in pieces)
    operands, inside, turned, turn_buf = [acts, grads, basis_in, basis_out], [], [], []
    if queries is not None:
        operands.append(queries)
        inside.append(beside)
        layers, count, depth = queries.shape
        turned = [jax.ShapeDtypeStruct((layers, depth, count), queries.dtype)] * 2
        turn_buf = [pltpu.VMEM(queries.shape, queries.dtype)]
    hbm = pl.BlockSpec(memory_space=pltpu.HBM)
    vmem = pl.BlockSpec(memory_space=pltpu.VMEM)

    def project_pairs(*refs):
        project(flips, groups, pieces, queries is not None, *refs)

    return pl.pallas_call(
        project_pairs,
        out_shape=turned
        + [
            jax.ShapeDtypeStruct((tokens + tokens // g, both), jnp.int16)
            if g
            else jax.ShapeDtypeStruct((tokens, both), jnp.float32)
            for g in groups
        ],
        in_specs=[hbm] * len(operands) + [vmem] * len(inside),
        out_specs=[vmem] * (len(turned) + len(groups)),
        scratch_shapes=turn_buf
        + [
            pltpu.VMEM((len(flips), tokens, width), acts.dtype),
            pltpu.VMEM((len(flips), tokens, width), grads.dtype),
            pltpu.VMEM((len(flips), *basis_in.shape[1:]), basis_in.dtype),
            pltpu.VMEM((len(flips), *basis_out.shape[1:]), basis_out.dtype),
            pltpu.VMEM((tokens // 16, both), jnp.float32),
            pltpu.SemaphoreType.DMA((2, steps)),
            pltpu.SemaphoreType.DMA((3, len(flips))),
        ],
        compiler_params=pltpu.CompilerParams(vmem_limit_bytes=VMEM),
    )(*(pltpu.with_memory_space_constraint(x, pltpu.HBM) for x in operands), *inside)


def decode(ref, tokens):
    shared = ref.shape[0] - tokens
    both = ref.shape[1]
    log = ref[pl.ds(tokens, shared), :].astype(jnp.int32).astype(jnp.float32)
    scale = jnp.exp2(log * (1.0 / STEPS)) * (1.0 / TOP)
    codes = ref[pl.ds(0, tokens), :].astype(jnp.int32).astype(jnp.float32)
    return (codes.reshape(shared, tokens // shared, both) * scale[:, None, :]).reshape(tokens, both)


def add_up(total, partial, out):
    out[...] = total[...] + decode(partial, total.shape[0])


def outer(lengths, most, last, out, grad):
    tokens, both = most.shape
    half = both // 2
    example = lax.axis_index("tensor") % lengths.shape[0]
    count = lengths[example]
    total = most[...] + decode(last, tokens)
    row = lax.broadcasted_iota(jnp.int32, (tokens, both), 0)
    lane = lax.broadcasted_iota(jnp.int32, (1, both), 1)
    weight = jnp.where(lane < half, 1.0 / jnp.full((1, both), count, jnp.int32).astype(jnp.float32), 1.0)
    weighted = jnp.where(row < count, total * weight, 0.0)
    first = weighted.astype(jnp.bfloat16)
    rest = (weighted - first.astype(jnp.float32)).astype(jnp.bfloat16)
    wide = tn(first, jnp.concatenate([first, rest], axis=1))
    product = wide[:, :both] + (wide[:, both:] + tn(rest, first))
    grad[...] = product[:half, :]
    even = grad[pl.ds(0, half // 2, stride=2), :][:, half:]
    odd = grad[pl.ds(1, half // 2, stride=2), :][:, half:]
    blocks = jnp.concatenate([even, odd], axis=1)
    block_rows = blocks.shape[0] // 2
    for t in range(4):
        for x in range(2):
            out[t * 2 + x] = blocks[x * block_rows : (x + 1) * block_rows]


def through_fisher(grads, fisher, beside, out):
    layers, _, width = fisher.shape
    lanes = grads.shape[2]
    rows = grads.shape[0] // layers
    depth = grads.shape[1] * lanes // 2
    cut = out.shape[2]
    halves = width // cut
    core = lax.axis_index("core")
    steps = depth // lanes
    order = [e * 2 + x for x in range(2) for e in range(rows // 2)]
    every = []
    for layer in range(layers):
        mapped = None
        for block, owner in ((fisher, core), (beside, 1 - core)):
            parts = [
                jnp.concatenate([grads[layer * rows + s, pl.ds(owner * steps + r, 1), :] for s in order], axis=0)
                for r in range(steps)
            ]
            term = nn(thirds(jnp.concatenate(parts, axis=1)), block[layer, pl.ds(0, depth), :])
            mapped = term if mapped is None else mapped + term
        every.append(add_thirds(mapped))
    for x in range(2):
        own = jnp.concatenate([mapped[x * rows // 2 : (x + 1) * rows // 2] for mapped in every], axis=0)
        mapped = jnp.concatenate([own[:, h * cut : (h + 1) * cut] for h in range(halves)], axis=0)
        for t in range(4):
            out[t * 2 + x] = mapped


def with_queries(mapped, own, beside, across, corner, out):
    layers, depth, count = own.shape
    halves = depth // mapped.shape[2]
    rows = mapped.shape[1] // halves
    here = lax.axis_index("x") * 2 + lax.axis_index("core")
    sums = [None] * layers
    for k, block in enumerate((own, beside, across, corner)):
        both = mapped[(here ^ k) * 2] + mapped[(here ^ k) * 2 + 1]
        left = thirds(jnp.concatenate([both[h * rows : (h + 1) * rows] for h in range(halves)], axis=1))
        for layer in range(layers):
            term = nn(left, block[layer]) if k < 2 else nt(left, block[layer])
            sums[layer] = term if sums[layer] is None else sums[layer] + term
    examples = rows // layers
    result = None
    for layer in range(layers):
        scores = add_thirds(sums[layer])[layer * examples : (layer + 1) * examples]
        result = scores if result is None else result + scores
    out[...] = result


def swap(x, axis, flip):
    return lax.ppermute(x, axis, [(i, i ^ flip) for i in range(lax.axis_size(axis))])


def in_vmem(x):
    return pltpu.with_memory_space_constraint(x, pltpu.VMEM)


def small(acts_in, grads_out, basis_in, basis_out, lengths, fisher_inv, queries):
    vmem = pl.BlockSpec(memory_space=pltpu.VMEM)
    params = pltpu.CompilerParams(vmem_limit_bytes=VMEM)
    proj_width = basis_in.shape[2]
    operands = (acts_in, grads_out, jnp.swapaxes(basis_in, 1, 2), jnp.swapaxes(basis_out, 1, 2))

    across, beside = swap(queries, "x", 1), swap(queries, "core", 1)
    (far,) = projector((3,), (32,), PIECES_ONE, *operands)
    acts_in, grads_out, far = lax.optimization_barrier((acts_in, grads_out, far))
    middle, near = projector((2, 1), (32, 32), PIECES_TWO, acts_in, grads_out, *operands[2:])
    acts_in, middle, near = lax.optimization_barrier((acts_in, middle, near))
    queries, beside, here = projector((0,), (0,), PIECES_ONE, acts_in, grads_out, *operands[2:], queries, beside)
    far, middle = swap(far, "tensor", 3), swap(middle, "tensor", 2)
    near = swap(near, "tensor", 1)
    fisher_beside = swap(fisher_inv, "core", 1)

    for partial in (far, middle):
        here = pl.pallas_call(
            add_up,
            out_shape=jax.ShapeDtypeStruct(here.shape, jnp.float32),
            in_specs=[vmem] * 2,
            out_specs=vmem,
            compiler_params=params,
        )(here, partial)

    blocks = pl.pallas_call(
        outer,
        out_shape=jax.ShapeDtypeStruct((8, proj_width // 4, 2 * proj_width), jnp.float32),
        in_specs=[pl.BlockSpec(memory_space=pltpu.SMEM)] + [vmem] * 2,
        out_specs=vmem,
        scratch_shapes=[pltpu.VMEM((proj_width, 2 * proj_width), jnp.float32)],
        compiler_params=params,
    )(lengths, here, near)
    blocks, fisher_beside = lax.optimization_barrier((blocks, fisher_beside))
    blocks = lax.all_to_all(blocks, ("tensor", "x"), 0, 0, tiled=True)

    mapped = pl.pallas_call(
        through_fisher,
        out_shape=jax.ShapeDtypeStruct((8, 8, fisher_inv.shape[2] // 2), jnp.float32),
        in_specs=[vmem] * 3,
        out_specs=vmem,
        compiler_params=params,
    )(blocks, in_vmem(fisher_inv), in_vmem(fisher_beside))
    across, mapped = lax.optimization_barrier((across, mapped))
    corner = swap(across, "core", 1)
    mapped = lax.all_to_all(mapped, ("tensor", "x"), 0, 0, tiled=True)

    return pl.pallas_call(
        with_queries,
        out_shape=jax.ShapeDtypeStruct((acts_in.shape[1], queries.shape[2]), jnp.float32),
        in_specs=[vmem] * 5,
        out_specs=vmem,
        compiler_params=params,
    )(mapped, queries, beside, across, corner)


def general(acts_in, grads_out, basis_in, basis_out, lengths, fisher_inv, queries):
    proj_width = basis_in.shape[2]
    layer_count = acts_in.shape[0]
    local_examples = acts_in.shape[1]
    proj_in = jnp.einsum("letd,ldr->letr", acts_in, basis_in, preferred_element_type=jnp.float32)
    proj_out = jnp.einsum(
        "letd,ldr->letr", grads_out, basis_out, preferred_element_type=jnp.float32
    )
    partial_proj = jnp.concatenate([proj_out, proj_in], axis=3)
    summed_proj = lax.psum(partial_proj, "tensor")
    share_len = summed_proj.shape[2]
    proj_out = summed_proj[..., :proj_width]
    proj_in = summed_proj[..., proj_width:]
    positions = lax.broadcasted_iota(jnp.int32, (share_len,), 0)
    token_weight = jnp.where(positions[None, :] < lengths[:, None], 1.0, 0.0).astype(jnp.float32)
    token_weight = token_weight / lengths[:, None].astype(jnp.float32)
    weighted = proj_out * token_weight[None, :, :, None]
    outer_prod = jnp.einsum("leta,letb->leab", weighted, proj_in, precision=lax.Precision.HIGHEST)
    example_grads = outer_prod.reshape(layer_count, local_examples, proj_width * proj_width)
    row_blocks = lax.all_to_all(example_grads, "dp", split_axis=2, concat_axis=1, tiled=True)
    gathered_queries = lax.all_gather(queries, "dp", axis=2, tiled=True)
    mapped = jnp.einsum(
        "lqj,lij->lqi",
        gathered_queries,
        lax.all_gather(fisher_inv, "tensor", axis=2, tiled=True),
        preferred_element_type=jnp.float32,
    )
    score_terms = jnp.einsum("lei,lqi->eq", row_blocks, mapped, precision=lax.Precision.HIGHEST)
    return lax.psum_scatter(score_terms, "dp", scatter_dimension=0, tiled=True)


def solution(mesh):
    dp = ("dp",)
    local = general
    if (mesh.shape["parts"], mesh.shape["tensor"], mesh.shape["dp"]) == (2, 4, 4):
        mesh = jax.sharding.Mesh(mesh.devices.reshape(2, 4, 2, 2), ("parts", "tensor", "x", "core"))
        dp = ("x", "core")
        local = small
    in_specs = (
        P(None, ("parts", *dp), None, "tensor"),
        P(None, ("parts", *dp), None, "tensor"),
        P(None, "tensor", None),
        P(None, "tensor", None),
        P(("parts", *dp)),
        P(None, dp, "tensor"),
        P(None, "tensor", dp),
    )
    out_specs = P(("parts", *dp), "tensor")
    return jax.shard_map(local, mesh=mesh, in_specs=in_specs, out_specs=out_specs, check_vma=False)
```

```python
import jax
import jax.numpy as jnp
from jax import lax
from jax.experimental import pallas as pl
from jax.experimental.pallas import tpu as pltpu
from jax.sharding import PartitionSpec as P

STEPS = 64.0
TOP = 32767.0
PIECES_TWO = ((128, 384), (256, 256))
PIECES_ONE = ((128, 384),)
AHEAD = 2
VMEM = 24 * 1024 * 1024


def nn(a, b):
    return lax.dot_general(a, b, (((1,), (0,)), ((), ())), preferred_element_type=jnp.float32)


def nt(a, b):
    return lax.dot_general(a, b, (((1,), (1,)), ((), ())), preferred_element_type=jnp.float32)


def tn(a, b):
    return lax.dot_general(a, b, (((0,), (0,)), ((), ())), preferred_element_type=jnp.float32)


def thirds(x):
    first = x.astype(jnp.bfloat16).astype(jnp.float32)
    rest = x - first
    second = rest.astype(jnp.bfloat16).astype(jnp.float32)
    return jnp.concatenate([first, second, rest - second], axis=0).astype(jnp.bfloat16)


def add_thirds(x):
    rows = x.shape[0] // 3
    return x[:rows] + (x[rows : 2 * rows] + x[2 * rows :])


def project(flips, groups, pieces, turn, acts, grads, basis_in, basis_out, *refs):
    *refs, a_buf, g_buf, in_buf, out_buf, scale_log, sems, basis_sems = refs
    queries = beside = lengths = turned = turned_beside = weights = turn_buf = None
    if turn:
        *refs, turn_buf = refs
        queries, beside, lengths, turned, turned_beside, weights, *refs = refs
    outs = refs
    examples, tokens = acts.shape[1], acts.shape[2]
    here = lax.axis_index("tensor")
    layers = [(here ^ flip) // examples for flip in flips]
    first = []
    for k, layer in enumerate(layers):
        first.append(pltpu.make_async_copy(basis_out.at[layer], out_buf.at[k], basis_sems.at[0, k]))
        first.append(pltpu.make_async_copy(basis_in.at[layer], in_buf.at[k], basis_sems.at[1, k]))
    if turn:
        first.append(pltpu.make_async_copy(queries, turn_buf, basis_sems.at[2, 0]))
    copies, spans = [], []
    for k, flip in enumerate(flips):
        example = (here ^ flip) % examples
        begin = 0
        for size in pieces[k]:
            rows, at = pl.ds(begin, size), len(copies)
            spans.append((k, begin, size))
            copies.append(
                (
                    pltpu.make_async_copy(grads.at[layers[k], example, rows, :], g_buf.at[k, rows, :], sems.at[0, at]),
                    pltpu.make_async_copy(acts.at[layers[k], example, rows, :], a_buf.at[k, rows, :], sems.at[1, at]),
                )
            )
            begin += size
    for copy in first:
        copy.start()
    for c in range(AHEAD):
        for copy in copies[c]:
            copy.start()
    for copy in first:
        copy.wait()
    if turn:
        for i in range(turned.shape[0]):
            turned[i] = turn_buf[i].T
            turned_beside[i] = beside[i].T
        weigh(lengths, weights)
    for at, (k, begin, size) in enumerate(spans):
        group, out, rows = groups[k], outs[k], pl.ds(begin, size)
        for copy in copies[at]:
            copy.wait()
        if at + AHEAD < len(copies):
            for copy in copies[at + AHEAD]:
                copy.start()
        proj_out = nt(g_buf[k, rows, :], out_buf[k])
        proj_in = nt(a_buf[k, rows, :], in_buf[k])
        both = jnp.concatenate([proj_out, proj_in], axis=1)
        if not group:
            out[rows, :] = both
            continue
        grouped = both.reshape(size // group, group, both.shape[1])
        most = jnp.maximum(jnp.max(jnp.abs(grouped), axis=1), 1e-30)
        log = jnp.ceil(jnp.log2(most) * STEPS)
        scale = jnp.exp2(log * (-1.0 / STEPS)) * TOP
        codes = jnp.round(grouped * scale[:, None, :])
        codes = jnp.minimum(jnp.maximum(codes, -TOP), TOP).reshape(both.shape)
        out[rows, :] = codes.astype(jnp.int32).astype(jnp.int16)
        scale_log[pl.ds(begin // group, size // group), :] = log
        if begin + size == tokens:
            log = scale_log[pl.ds(0, tokens // group), :]
            out[pl.ds(tokens, tokens // group), :] = log.astype(jnp.int32).astype(jnp.int16)


def projector(flips, groups, pieces, acts, grads, basis_in, basis_out, queries=None, beside=None, lengths=None):
    tokens, width = acts.shape[2], acts.shape[3]
    both = 2 * basis_in.shape[1]
    steps = sum(len(p) for p in pieces)
    operands, inside, turned, turn_buf = [acts, grads, basis_in, basis_out], [], [], []
    if queries is not None:
        operands.append(queries)
        inside += [beside, lengths]
        layers, count, depth = queries.shape
        turned = [jax.ShapeDtypeStruct((layers, depth, count), queries.dtype)] * 2
        turned.append(jax.ShapeDtypeStruct((tokens, both), jnp.float32))
        turn_buf = [pltpu.VMEM(queries.shape, queries.dtype)]
    hbm = pl.BlockSpec(memory_space=pltpu.HBM)
    vmem, smem = pl.BlockSpec(memory_space=pltpu.VMEM), pl.BlockSpec(memory_space=pltpu.SMEM)

    def project_pairs(*refs):
        project(flips, groups, pieces, queries is not None, *refs)

    return pl.pallas_call(
        project_pairs,
        out_shape=turned
        + [
            jax.ShapeDtypeStruct((tokens + tokens // g, both), jnp.int16)
            if g
            else jax.ShapeDtypeStruct((tokens, both), jnp.float32)
            for g in groups
        ],
        in_specs=[hbm] * len(operands) + [vmem, smem][: len(inside)],
        out_specs=[vmem] * (len(turned) + len(groups)),
        scratch_shapes=turn_buf
        + [
            pltpu.VMEM((len(flips), tokens, width), acts.dtype),
            pltpu.VMEM((len(flips), tokens, width), grads.dtype),
            pltpu.VMEM((len(flips), *basis_in.shape[1:]), basis_in.dtype),
            pltpu.VMEM((len(flips), *basis_out.shape[1:]), basis_out.dtype),
            pltpu.VMEM((tokens // 16, both), jnp.float32),
            pltpu.SemaphoreType.DMA((2, steps)),
            pltpu.SemaphoreType.DMA((3, len(flips))),
        ],
        compiler_params=pltpu.CompilerParams(vmem_limit_bytes=VMEM),
    )(*(pltpu.with_memory_space_constraint(x, pltpu.HBM) for x in operands), *inside)


def decode(ref, tokens):
    shared = ref.shape[0] - tokens
    both = ref.shape[1]
    log = ref[pl.ds(tokens, shared), :].astype(jnp.int32).astype(jnp.float32)
    scale = jnp.exp2(log * (1.0 / STEPS)) * (1.0 / TOP)
    codes = ref[pl.ds(0, tokens), :].astype(jnp.int32).astype(jnp.float32)
    return (codes.reshape(shared, tokens // shared, both) * scale[:, None, :]).reshape(tokens, both)


def add_up(total, partial, out):
    out[...] = total[...] + decode(partial, total.shape[0])


def weigh(lengths, weights):
    tokens, both = weights.shape
    count = lengths[lax.axis_index("tensor") % lengths.shape[0]]
    row = lax.broadcasted_iota(jnp.int32, (tokens, both), 0)
    lane = lax.broadcasted_iota(jnp.int32, (1, both), 1)
    share = 1.0 / jnp.full((1, both), count, jnp.int32).astype(jnp.float32)
    weights[...] = jnp.where(row < count, jnp.where(lane < both // 2, share, 1.0), 0.0)


def outer(weights, most, last, out, grad):
    tokens, both = most.shape
    half = both // 2
    weighted = (most[...] + decode(last, tokens)) * weights[...]
    first = weighted.astype(jnp.bfloat16)
    rest = (weighted - first.astype(jnp.float32)).astype(jnp.bfloat16)
    wide = tn(first, jnp.concatenate([first, rest], axis=1))
    product = wide[:, :both] + (wide[:, both:] + tn(rest, first))
    grad[...] = product[:half, :]
    even = grad[pl.ds(0, half // 2, stride=2), :][:, half:]
    odd = grad[pl.ds(1, half // 2, stride=2), :][:, half:]
    blocks = jnp.concatenate([even, odd], axis=1)
    block_rows = blocks.shape[0] // 2
    for t in range(4):
        for x in range(2):
            out[t * 2 + x] = blocks[x * block_rows : (x + 1) * block_rows]


def through_fisher(grads, fisher, beside, out):
    layers, _, width = fisher.shape
    lanes = grads.shape[2]
    rows = grads.shape[0] // layers
    depth = grads.shape[1] * lanes // 2
    cut = out.shape[2]
    halves = width // cut
    core = lax.axis_index("core")
    steps = depth // lanes
    order = [e * 2 + x for x in range(2) for e in range(rows // 2)]
    every = []
    for layer in range(layers):
        mapped = None
        for block, owner in ((fisher, core), (beside, 1 - core)):
            parts = [
                jnp.concatenate([grads[layer * rows + s, pl.ds(owner * steps + r, 1), :] for s in order], axis=0)
                for r in range(steps)
            ]
            term = nn(thirds(jnp.concatenate(parts, axis=1)), block[layer, pl.ds(0, depth), :])
            mapped = term if mapped is None else mapped + term
        every.append(add_thirds(mapped))
    for x in range(2):
        own = jnp.concatenate([mapped[x * rows // 2 : (x + 1) * rows // 2] for mapped in every], axis=0)
        mapped = jnp.concatenate([own[:, h * cut : (h + 1) * cut] for h in range(halves)], axis=0)
        for t in range(4):
            out[t * 2 + x] = mapped


def with_queries(mapped, own, beside, across, corner, out):
    layers, depth, count = own.shape
    halves = depth // mapped.shape[2]
    rows = mapped.shape[1] // halves
    here = lax.axis_index("x") * 2 + lax.axis_index("core")
    sums = [None] * layers
    for k, block in enumerate((own, beside, across, corner)):
        both = mapped[(here ^ k) * 2] + mapped[(here ^ k) * 2 + 1]
        left = thirds(jnp.concatenate([both[h * rows : (h + 1) * rows] for h in range(halves)], axis=1))
        for layer in range(layers):
            term = nn(left, block[layer]) if k < 2 else nt(left, block[layer])
            sums[layer] = term if sums[layer] is None else sums[layer] + term
    examples = rows // layers
    result = None
    for layer in range(layers):
        scores = add_thirds(sums[layer])[layer * examples : (layer + 1) * examples]
        result = scores if result is None else result + scores
    out[...] = result


def swap(x, axis, flip):
    return lax.ppermute(x, axis, [(i, i ^ flip) for i in range(lax.axis_size(axis))])


def in_vmem(x):
    return pltpu.with_memory_space_constraint(x, pltpu.VMEM)


def small(acts_in, grads_out, basis_in, basis_out, lengths, fisher_inv, queries):
    vmem = pl.BlockSpec(memory_space=pltpu.VMEM)
    params = pltpu.CompilerParams(vmem_limit_bytes=VMEM)
    proj_width = basis_in.shape[2]
    operands = (acts_in, grads_out, jnp.swapaxes(basis_in, 1, 2), jnp.swapaxes(basis_out, 1, 2))

    across, beside = swap(queries, "x", 1), swap(queries, "core", 1)
    (far,) = projector((3,), (32,), PIECES_ONE, *operands)
    acts_in, grads_out, far = lax.optimization_barrier((acts_in, grads_out, far))
    middle, near = projector((2, 1), (32, 32), PIECES_TWO, acts_in, grads_out, *operands[2:])
    acts_in, middle, near = lax.optimization_barrier((acts_in, middle, near))
    queries, beside, weights, here = projector(
        (0,), (0,), PIECES_ONE, acts_in, grads_out, *operands[2:], queries, beside, lengths
    )
    far, middle = swap(far, "tensor", 3), swap(middle, "tensor", 2)
    near = swap(near, "tensor", 1)
    fisher_beside = swap(fisher_inv, "core", 1)

    for partial in (far, middle):
        here = pl.pallas_call(
            add_up,
            out_shape=jax.ShapeDtypeStruct(here.shape, jnp.float32),
            in_specs=[vmem] * 2,
            out_specs=vmem,
            compiler_params=params,
        )(here, partial)

    blocks = pl.pallas_call(
        outer,
        out_shape=jax.ShapeDtypeStruct((8, proj_width // 4, 2 * proj_width), jnp.float32),
        in_specs=[vmem] * 3,
        out_specs=vmem,
        scratch_shapes=[pltpu.VMEM((proj_width, 2 * proj_width), jnp.float32)],
        compiler_params=params,
    )(weights, here, near)
    blocks, fisher_beside = lax.optimization_barrier((blocks, fisher_beside))
    blocks = lax.all_to_all(blocks, ("tensor", "x"), 0, 0, tiled=True)

    mapped = pl.pallas_call(
        through_fisher,
        out_shape=jax.ShapeDtypeStruct((8, 8, fisher_inv.shape[2] // 2), jnp.float32),
        in_specs=[vmem] * 3,
        out_specs=vmem,
        compiler_params=params,
    )(blocks, in_vmem(fisher_inv), in_vmem(fisher_beside))
    across, mapped = lax.optimization_barrier((across, mapped))
    corner = swap(across, "core", 1)
    mapped = lax.all_to_all(mapped, ("tensor", "x"), 0, 0, tiled=True)

    return pl.pallas_call(
        with_queries,
        out_shape=jax.ShapeDtypeStruct((acts_in.shape[1], queries.shape[2]), jnp.float32),
        in_specs=[vmem] * 5,
        out_specs=vmem,
        compiler_params=params,
    )(mapped, queries, beside, across, corner)


def general(acts_in, grads_out, basis_in, basis_out, lengths, fisher_inv, queries):
    proj_width = basis_in.shape[2]
    layer_count = acts_in.shape[0]
    local_examples = acts_in.shape[1]
    proj_in = jnp.einsum("letd,ldr->letr", acts_in, basis_in, preferred_element_type=jnp.float32)
    proj_out = jnp.einsum(
        "letd,ldr->letr", grads_out, basis_out, preferred_element_type=jnp.float32
    )
    partial_proj = jnp.concatenate([proj_out, proj_in], axis=3)
    summed_proj = lax.psum(partial_proj, "tensor")
    share_len = summed_proj.shape[2]
    proj_out = summed_proj[..., :proj_width]
    proj_in = summed_proj[..., proj_width:]
    positions = lax.broadcasted_iota(jnp.int32, (share_len,), 0)
    token_weight = jnp.where(positions[None, :] < lengths[:, None], 1.0, 0.0).astype(jnp.float32)
    token_weight = token_weight / lengths[:, None].astype(jnp.float32)
    weighted = proj_out * token_weight[None, :, :, None]
    outer_prod = jnp.einsum("leta,letb->leab", weighted, proj_in, precision=lax.Precision.HIGHEST)
    example_grads = outer_prod.reshape(layer_count, local_examples, proj_width * proj_width)
    row_blocks = lax.all_to_all(example_grads, "dp", split_axis=2, concat_axis=1, tiled=True)
    gathered_queries = lax.all_gather(queries, "dp", axis=2, tiled=True)
    mapped = jnp.einsum(
        "lqj,lij->lqi",
        gathered_queries,
        lax.all_gather(fisher_inv, "tensor", axis=2, tiled=True),
        preferred_element_type=jnp.float32,
    )
    score_terms = jnp.einsum("lei,lqi->eq", row_blocks, mapped, precision=lax.Precision.HIGHEST)
    return lax.psum_scatter(score_terms, "dp", scatter_dimension=0, tiled=True)


def solution(mesh):
    dp = ("dp",)
    local = general
    if (mesh.shape["parts"], mesh.shape["tensor"], mesh.shape["dp"]) == (2, 4, 4):
        mesh = jax.sharding.Mesh(mesh.devices.reshape(2, 4, 2, 2), ("parts", "tensor", "x", "core"))
        dp = ("x", "core")
        local = small
    in_specs = (
        P(None, ("parts", *dp), None, "tensor"),
        P(None, ("parts", *dp), None, "tensor"),
        P(None, "tensor", None),
        P(None, "tensor", None),
        P(("parts", *dp)),
        P(None, dp, "tensor"),
        P(None, "tensor", dp),
    )
    out_specs = P(("parts", *dp), "tensor")
    return jax.shard_map(local, mesh=mesh, in_specs=in_specs, out_specs=out_specs, check_vma=False)
```

```python
import jax
import jax.numpy as jnp
from jax import lax
from jax.experimental import pallas as pl
from jax.experimental.pallas import tpu as pltpu
from jax.sharding import PartitionSpec as P

STEPS = 64.0
TOP = 32767.0
PIECES_TWO = ((128, 384), (256, 256))
PIECES_ONE = ((128, 384),)
AHEAD = 2
VMEM = 24 * 1024 * 1024


def nn(a, b):
    return lax.dot_general(a, b, (((1,), (0,)), ((), ())), preferred_element_type=jnp.float32)


def nt(a, b):
    return lax.dot_general(a, b, (((1,), (1,)), ((), ())), preferred_element_type=jnp.float32)


def tn(a, b):
    return lax.dot_general(a, b, (((0,), (0,)), ((), ())), preferred_element_type=jnp.float32)


def thirds(x):
    first = x.astype(jnp.bfloat16).astype(jnp.float32)
    rest = x - first
    second = rest.astype(jnp.bfloat16).astype(jnp.float32)
    return jnp.concatenate([first, second, rest - second], axis=0).astype(jnp.bfloat16)


def add_thirds(x):
    rows = x.shape[0] // 3
    return x[:rows] + (x[rows : 2 * rows] + x[2 * rows :])


def project(flips, groups, pieces, turn, acts, grads, basis_in, basis_out, *refs):
    *refs, a_buf, g_buf, in_buf, out_buf, scale_log, sems, basis_sems = refs
    queries = beside = lengths = turned = turned_beside = weights = turn_buf = None
    if turn:
        *refs, turn_buf = refs
        queries, beside, lengths, turned, turned_beside, weights, *refs = refs
    outs = refs
    examples, tokens = acts.shape[1], acts.shape[2]
    here = lax.axis_index("tensor")
    layers = [(here ^ flip) // examples for flip in flips]
    first = []
    for k, layer in enumerate(layers):
        first.append(pltpu.make_async_copy(basis_out.at[layer], out_buf.at[k], basis_sems.at[0, k]))
        first.append(pltpu.make_async_copy(basis_in.at[layer], in_buf.at[k], basis_sems.at[1, k]))
    if turn:
        first.append(pltpu.make_async_copy(queries, turn_buf, basis_sems.at[2, 0]))
    copies, spans = [], []
    for k, flip in enumerate(flips):
        example = (here ^ flip) % examples
        begin = 0
        for size in pieces[k]:
            rows, at = pl.ds(begin, size), len(copies)
            spans.append((k, begin, size))
            copies.append(
                (
                    pltpu.make_async_copy(grads.at[layers[k], example, rows, :], g_buf.at[k, rows, :], sems.at[0, at]),
                    pltpu.make_async_copy(acts.at[layers[k], example, rows, :], a_buf.at[k, rows, :], sems.at[1, at]),
                )
            )
            begin += size
    for copy in first:
        copy.start()
    for c in range(AHEAD):
        for copy in copies[c]:
            copy.start()
    for copy in first:
        copy.wait()
    if turn:
        for i in range(turned.shape[0]):
            turned[i] = turn_buf[i].T
            turned_beside[i] = beside[i].T
        weigh(lengths, weights)
    for at, (k, begin, size) in enumerate(spans):
        group, out, rows = groups[k], outs[k], pl.ds(begin, size)
        for copy in copies[at]:
            copy.wait()
        if at + AHEAD < len(copies):
            for copy in copies[at + AHEAD]:
                copy.start()
        proj_out = nt(g_buf[k, rows, :], out_buf[k])
        proj_in = nt(a_buf[k, rows, :], in_buf[k])
        both = jnp.concatenate([proj_out, proj_in], axis=1)
        if not group:
            out[rows, :] = both
            continue
        grouped = both.reshape(size // group, group, both.shape[1])
        most = jnp.maximum(jnp.max(jnp.abs(grouped), axis=1), 1e-30)
        log = jnp.ceil(jnp.log2(most) * STEPS)
        scale = jnp.exp2(log * (-1.0 / STEPS)) * TOP
        codes = jnp.round(grouped * scale[:, None, :])
        codes = jnp.minimum(jnp.maximum(codes, -TOP), TOP).reshape(both.shape)
        out[rows, :] = codes.astype(jnp.int32).astype(jnp.int16)
        scale_log[pl.ds(begin // group, size // group), :] = log
        if begin + size == tokens:
            log = scale_log[pl.ds(0, tokens // group), :]
            out[pl.ds(tokens, tokens // group), :] = log.astype(jnp.int32).astype(jnp.int16)


def projector(flips, groups, pieces, acts, grads, basis_in, basis_out, queries=None, beside=None, lengths=None):
    tokens, width = acts.shape[2], acts.shape[3]
    both = 2 * basis_in.shape[1]
    steps = sum(len(p) for p in pieces)
    operands, inside, turned, turn_buf = [acts, grads, basis_in, basis_out], [], [], []
    if queries is not None:
        operands.append(queries)
        inside += [beside, lengths]
        layers, count, depth = queries.shape
        turned = [jax.ShapeDtypeStruct((layers, depth, count), queries.dtype)] * 2
        turned.append(jax.ShapeDtypeStruct((tokens, both), jnp.float32))
        turn_buf = [pltpu.VMEM(queries.shape, queries.dtype)]
    hbm = pl.BlockSpec(memory_space=pltpu.HBM)
    vmem, smem = pl.BlockSpec(memory_space=pltpu.VMEM), pl.BlockSpec(memory_space=pltpu.SMEM)

    def project_pairs(*refs):
        project(flips, groups, pieces, queries is not None, *refs)

    return pl.pallas_call(
        project_pairs,
        out_shape=turned
        + [
            jax.ShapeDtypeStruct((tokens + tokens // g, both), jnp.int16)
            if g
            else jax.ShapeDtypeStruct((tokens, both), jnp.float32)
            for g in groups
        ],
        in_specs=[hbm] * len(operands) + [vmem, smem][: len(inside)],
        out_specs=[vmem] * (len(turned) + len(groups)),
        scratch_shapes=turn_buf
        + [
            pltpu.VMEM((len(flips), tokens, width), acts.dtype),
            pltpu.VMEM((len(flips), tokens, width), grads.dtype),
            pltpu.VMEM((len(flips), *basis_in.shape[1:]), basis_in.dtype),
            pltpu.VMEM((len(flips), *basis_out.shape[1:]), basis_out.dtype),
            pltpu.VMEM((tokens // 16, both), jnp.float32),
            pltpu.SemaphoreType.DMA((2, steps)),
            pltpu.SemaphoreType.DMA((3, len(flips))),
        ],
        compiler_params=pltpu.CompilerParams(vmem_limit_bytes=VMEM),
    )(*(pltpu.with_memory_space_constraint(x, pltpu.HBM) for x in operands), *inside)


def decode(ref, tokens):
    shared = ref.shape[0] - tokens
    both = ref.shape[1]
    log = ref[pl.ds(tokens, shared), :].astype(jnp.int32).astype(jnp.float32)
    scale = jnp.exp2(log * (1.0 / STEPS)) * (1.0 / TOP)
    codes = ref[pl.ds(0, tokens), :].astype(jnp.int32).astype(jnp.float32)
    return (codes.reshape(shared, tokens // shared, both) * scale[:, None, :]).reshape(tokens, both)


def add_up(total, partial, out):
    out[...] = total[...] + decode(partial, total.shape[0])


def weigh(lengths, weights):
    tokens, both = weights.shape
    count = lengths[lax.axis_index("tensor") % lengths.shape[0]]
    row = lax.broadcasted_iota(jnp.int32, (tokens, both), 0)
    lane = lax.broadcasted_iota(jnp.int32, (1, both), 1)
    share = 1.0 / jnp.full((1, both), count, jnp.int32).astype(jnp.float32)
    weights[...] = jnp.where(row < count, jnp.where(lane < both // 2, share, 1.0), 0.0)


def outer(weights, most, last, out, grad):
    tokens, both = most.shape
    half = both // 2
    weighted = (most[...] + decode(last, tokens)) * weights[...]
    first = weighted.astype(jnp.bfloat16)
    rest = (weighted - first.astype(jnp.float32)).astype(jnp.bfloat16)
    wide = tn(first, jnp.concatenate([first, rest], axis=1))
    product = wide[:, :both] + (wide[:, both:] + tn(rest, first))
    grad[...] = product[:half, :]
    even = grad[pl.ds(0, half // 2, stride=2), :][:, half:]
    odd = grad[pl.ds(1, half // 2, stride=2), :][:, half:]
    blocks = jnp.concatenate([even, odd], axis=1)
    block_rows = blocks.shape[0] // 2
    for t in range(4):
        for x in range(2):
            out[t * 2 + x] = blocks[x * block_rows : (x + 1) * block_rows]


def through_fisher(grads, fisher, beside, out):
    layers, _, width = fisher.shape
    lanes = grads.shape[2]
    rows = grads.shape[0] // layers
    depth = grads.shape[1] * lanes // 2
    core = lax.axis_index("core")
    steps = depth // lanes
    order = [e * 2 + x for x in range(2) for e in range(rows // 2)]
    every = []
    for layer in range(layers):
        mapped = None
        for block, owner in ((fisher, core), (beside, 1 - core)):
            parts = [
                jnp.concatenate([grads[layer * rows + s, pl.ds(owner * steps + r, 1), :] for s in order], axis=0)
                for r in range(steps)
            ]
            term = nn(thirds(jnp.concatenate(parts, axis=1)), block[layer, pl.ds(0, depth), :])
            mapped = term if mapped is None else mapped + term
        every.append(add_thirds(mapped))
    for x in range(2):
        own = jnp.concatenate([mapped[x * rows // 2 : (x + 1) * rows // 2] for mapped in every], axis=0)
        log = jnp.ceil(jnp.log2(jnp.maximum(jnp.max(jnp.abs(own), axis=1, keepdims=True), 1e-30)) * STEPS)
        codes = jnp.round(own * (jnp.exp2(log * (-1.0 / STEPS)) * TOP))
        codes = jnp.minimum(jnp.maximum(codes, -TOP), TOP)
        shared = jnp.broadcast_to(log, (own.shape[0], lanes))
        pieces = [codes[:, at : at + lanes] for at in range(0, width, lanes)] + [shared]
        rest = out.shape[1] - own.shape[0] * len(pieces)
        message = jnp.concatenate([*pieces, jnp.zeros((rest, lanes), jnp.float32)], axis=0)
        message = message.astype(jnp.int32).astype(jnp.int16)
        for t in range(4):
            out[t * 2 + x] = message


def with_queries(mapped, own, beside, across, corner, out):
    layers, depth, count = own.shape
    lanes = mapped.shape[2]
    examples = out.shape[0]
    rows = layers * examples
    here = lax.axis_index("x") * 2 + lax.axis_index("core")

    def read(source):
        message = mapped[source].astype(jnp.int32).astype(jnp.float32)
        last = depth // lanes * rows
        scale = jnp.exp2(message[last : last + rows] * (1.0 / STEPS)) * (1.0 / TOP)
        return jnp.concatenate([message[at : at + rows] * scale for at in range(0, last, rows)], axis=1)

    sums = [None] * layers
    for k, block in enumerate((own, beside, across, corner)):
        left = thirds(read((here ^ k) * 2) + read((here ^ k) * 2 + 1))
        for layer in range(layers):
            term = nn(left, block[layer]) if k < 2 else nt(left, block[layer])
            sums[layer] = term if sums[layer] is None else sums[layer] + term
    result = None
    for layer in range(layers):
        scores = add_thirds(sums[layer])[layer * examples : (layer + 1) * examples]
        result = scores if result is None else result + scores
    out[...] = result


def swap(x, axis, flip):
    return lax.ppermute(x, axis, [(i, i ^ flip) for i in range(lax.axis_size(axis))])


def in_vmem(x):
    return pltpu.with_memory_space_constraint(x, pltpu.VMEM)


def small(acts_in, grads_out, basis_in, basis_out, lengths, fisher_inv, queries):
    vmem = pl.BlockSpec(memory_space=pltpu.VMEM)
    params = pltpu.CompilerParams(vmem_limit_bytes=VMEM)
    proj_width = basis_in.shape[2]
    operands = (acts_in, grads_out, jnp.swapaxes(basis_in, 1, 2), jnp.swapaxes(basis_out, 1, 2))

    across, beside = swap(queries, "x", 1), swap(queries, "core", 1)
    (far,) = projector((3,), (32,), PIECES_ONE, *operands)
    acts_in, grads_out, far = lax.optimization_barrier((acts_in, grads_out, far))
    middle, near = projector((2, 1), (32, 32), PIECES_TWO, acts_in, grads_out, *operands[2:])
    acts_in, middle, near = lax.optimization_barrier((acts_in, middle, near))
    queries, beside, weights, here = projector(
        (0,), (0,), PIECES_ONE, acts_in, grads_out, *operands[2:], queries, beside, lengths
    )
    far, middle = swap(far, "tensor", 3), swap(middle, "tensor", 2)
    near = swap(near, "tensor", 1)
    fisher_beside = swap(fisher_inv, "core", 1)

    for partial in (far, middle):
        here = pl.pallas_call(
            add_up,
            out_shape=jax.ShapeDtypeStruct(here.shape, jnp.float32),
            in_specs=[vmem] * 2,
            out_specs=vmem,
            compiler_params=params,
        )(here, partial)

    blocks = pl.pallas_call(
        outer,
        out_shape=jax.ShapeDtypeStruct((8, proj_width // 4, 2 * proj_width), jnp.float32),
        in_specs=[vmem] * 3,
        out_specs=vmem,
        scratch_shapes=[pltpu.VMEM((proj_width, 2 * proj_width), jnp.float32)],
        compiler_params=params,
    )(weights, here, near)
    blocks, fisher_beside = lax.optimization_barrier((blocks, fisher_beside))
    blocks = lax.all_to_all(blocks, ("tensor", "x"), 0, 0, tiled=True)

    mapped = pl.pallas_call(
        through_fisher,
        out_shape=jax.ShapeDtypeStruct((8, 48, 128), jnp.int16),
        in_specs=[vmem] * 3,
        out_specs=vmem,
        compiler_params=params,
    )(blocks, in_vmem(fisher_inv), in_vmem(fisher_beside))
    across, mapped = lax.optimization_barrier((across, mapped))
    corner = swap(across, "core", 1)
    mapped = lax.all_to_all(mapped, ("tensor", "x"), 0, 0, tiled=True)

    return pl.pallas_call(
        with_queries,
        out_shape=jax.ShapeDtypeStruct((acts_in.shape[1], queries.shape[2]), jnp.float32),
        in_specs=[vmem] * 5,
        out_specs=vmem,
        compiler_params=params,
    )(mapped, queries, beside, across, corner)


def general(acts_in, grads_out, basis_in, basis_out, lengths, fisher_inv, queries):
    proj_width = basis_in.shape[2]
    layer_count = acts_in.shape[0]
    local_examples = acts_in.shape[1]
    proj_in = jnp.einsum("letd,ldr->letr", acts_in, basis_in, preferred_element_type=jnp.float32)
    proj_out = jnp.einsum(
        "letd,ldr->letr", grads_out, basis_out, preferred_element_type=jnp.float32
    )
    partial_proj = jnp.concatenate([proj_out, proj_in], axis=3)
    summed_proj = lax.psum(partial_proj, "tensor")
    share_len = summed_proj.shape[2]
    proj_out = summed_proj[..., :proj_width]
    proj_in = summed_proj[..., proj_width:]
    positions = lax.broadcasted_iota(jnp.int32, (share_len,), 0)
    token_weight = jnp.where(positions[None, :] < lengths[:, None], 1.0, 0.0).astype(jnp.float32)
    token_weight = token_weight / lengths[:, None].astype(jnp.float32)
    weighted = proj_out * token_weight[None, :, :, None]
    outer_prod = jnp.einsum("leta,letb->leab", weighted, proj_in, precision=lax.Precision.HIGHEST)
    example_grads = outer_prod.reshape(layer_count, local_examples, proj_width * proj_width)
    row_blocks = lax.all_to_all(example_grads, "dp", split_axis=2, concat_axis=1, tiled=True)
    gathered_queries = lax.all_gather(queries, "dp", axis=2, tiled=True)
    mapped = jnp.einsum(
        "lqj,lij->lqi",
        gathered_queries,
        lax.all_gather(fisher_inv, "tensor", axis=2, tiled=True),
        preferred_element_type=jnp.float32,
    )
    score_terms = jnp.einsum("lei,lqi->eq", row_blocks, mapped, precision=lax.Precision.HIGHEST)
    return lax.psum_scatter(score_terms, "dp", scatter_dimension=0, tiled=True)


def solution(mesh):
    dp = ("dp",)
    local = general
    if (mesh.shape["parts"], mesh.shape["tensor"], mesh.shape["dp"]) == (2, 4, 4):
        mesh = jax.sharding.Mesh(mesh.devices.reshape(2, 4, 2, 2), ("parts", "tensor", "x", "core"))
        dp = ("x", "core")
        local = small
    in_specs = (
        P(None, ("parts", *dp), None, "tensor"),
        P(None, ("parts", *dp), None, "tensor"),
        P(None, "tensor", None),
        P(None, "tensor", None),
        P(("parts", *dp)),
        P(None, dp, "tensor"),
        P(None, "tensor", dp),
    )
    out_specs = P(("parts", *dp), "tensor")
    return jax.shard_map(local, mesh=mesh, in_specs=in_specs, out_specs=out_specs, check_vma=False)
```

```python
import jax
import jax.numpy as jnp
from jax import lax
from jax.experimental import pallas as pl
from jax.experimental.pallas import tpu as pltpu
from jax.sharding import PartitionSpec as P

STEPS = 64.0
TOP = 32767.0
PIECES_TWO = ((128, 384), (256, 256))
PIECES_ONE = ((128, 384),)
AHEAD = 2
VMEM = 24 * 1024 * 1024


def nn(a, b):
    return lax.dot_general(a, b, (((1,), (0,)), ((), ())), preferred_element_type=jnp.float32)


def nt(a, b):
    return lax.dot_general(a, b, (((1,), (1,)), ((), ())), preferred_element_type=jnp.float32)


def tn(a, b):
    return lax.dot_general(a, b, (((0,), (0,)), ((), ())), preferred_element_type=jnp.float32)


def thirds(x):
    first = x.astype(jnp.bfloat16).astype(jnp.float32)
    rest = x - first
    second = rest.astype(jnp.bfloat16).astype(jnp.float32)
    return jnp.concatenate([first, second, rest - second], axis=0).astype(jnp.bfloat16)


def add_thirds(x):
    rows = x.shape[0] // 3
    return x[:rows] + (x[rows : 2 * rows] + x[2 * rows :])


def project(flips, groups, pieces, turn, acts, grads, basis_in, basis_out, *refs):
    *refs, a_buf, g_buf, in_buf, out_buf, scale_log, sems, basis_sems = refs
    queries = beside = lengths = turned = turned_beside = weights = turn_buf = None
    if turn:
        *refs, turn_buf = refs
        queries, beside, lengths, turned, turned_beside, weights, *refs = refs
    outs = refs
    examples, tokens = acts.shape[1], acts.shape[2]
    here = lax.axis_index("tensor")
    layers = [(here ^ flip) // examples for flip in flips]
    first = []
    for k, layer in enumerate(layers):
        first.append(pltpu.make_async_copy(basis_out.at[layer], out_buf.at[k], basis_sems.at[0, k]))
        first.append(pltpu.make_async_copy(basis_in.at[layer], in_buf.at[k], basis_sems.at[1, k]))
    if turn:
        first.append(pltpu.make_async_copy(queries, turn_buf, basis_sems.at[2, 0]))
    copies, spans = [], []
    for k, flip in enumerate(flips):
        example = (here ^ flip) % examples
        begin = 0
        for size in pieces[k]:
            rows, at = pl.ds(begin, size), len(copies)
            spans.append((k, begin, size))
            copies.append(
                (
                    pltpu.make_async_copy(grads.at[layers[k], example, rows, :], g_buf.at[k, rows, :], sems.at[0, at]),
                    pltpu.make_async_copy(acts.at[layers[k], example, rows, :], a_buf.at[k, rows, :], sems.at[1, at]),
                )
            )
            begin += size
    for copy in first:
        copy.start()
    for c in range(AHEAD):
        for copy in copies[c]:
            copy.start()
    for copy in first:
        copy.wait()
    if turn:
        for i in range(turned.shape[0]):
            turned[i] = turn_buf[i].T
            turned_beside[i] = beside[i].T
        weigh(lengths, weights)
    for at, (k, begin, size) in enumerate(spans):
        group, out, rows = groups[k], outs[k], pl.ds(begin, size)
        for copy in copies[at]:
            copy.wait()
        if at + AHEAD < len(copies):
            for copy in copies[at + AHEAD]:
                copy.start()
        proj_out = nt(g_buf[k, rows, :], out_buf[k])
        proj_in = nt(a_buf[k, rows, :], in_buf[k])
        both = jnp.concatenate([proj_out, proj_in], axis=1)
        if not group:
            out[rows, :] = both
            continue
        grouped = both.reshape(size // group, group, both.shape[1])
        most = jnp.maximum(jnp.max(jnp.abs(grouped), axis=1), 1e-30)
        log = jnp.ceil(jnp.log2(most) * STEPS)
        scale = jnp.exp2(log * (-1.0 / STEPS)) * TOP
        codes = jnp.round(grouped * scale[:, None, :])
        codes = jnp.minimum(jnp.maximum(codes, -TOP), TOP).reshape(both.shape)
        out[rows, :] = codes.astype(jnp.int32).astype(jnp.int16)
        scale_log[pl.ds(begin // group, size // group), :] = log
        if begin + size == tokens:
            log = scale_log[pl.ds(0, tokens // group), :]
            out[pl.ds(tokens, tokens // group), :] = log.astype(jnp.int32).astype(jnp.int16)


def projector(flips, groups, pieces, acts, grads, basis_in, basis_out, queries=None, beside=None, lengths=None):
    tokens, width = acts.shape[2], acts.shape[3]
    both = 2 * basis_in.shape[1]
    steps = sum(len(p) for p in pieces)
    operands, inside, turned, turn_buf = [acts, grads, basis_in, basis_out], [], [], []
    if queries is not None:
        operands.append(queries)
        inside += [beside, lengths]
        layers, count, depth = queries.shape
        turned = [jax.ShapeDtypeStruct((layers, depth, count), queries.dtype)] * 2
        turned.append(jax.ShapeDtypeStruct((tokens, both), jnp.float32))
        turn_buf = [pltpu.VMEM(queries.shape, queries.dtype)]
    hbm = pl.BlockSpec(memory_space=pltpu.HBM)
    vmem, smem = pl.BlockSpec(memory_space=pltpu.VMEM), pl.BlockSpec(memory_space=pltpu.SMEM)

    def project_pairs(*refs):
        project(flips, groups, pieces, queries is not None, *refs)

    return pl.pallas_call(
        project_pairs,
        out_shape=turned
        + [
            jax.ShapeDtypeStruct((tokens + tokens // g, both), jnp.int16)
            if g
            else jax.ShapeDtypeStruct((tokens, both), jnp.float32)
            for g in groups
        ],
        in_specs=[hbm] * len(operands) + [vmem, smem][: len(inside)],
        out_specs=[vmem] * (len(turned) + len(groups)),
        scratch_shapes=turn_buf
        + [
            pltpu.VMEM((len(flips), tokens, width), acts.dtype),
            pltpu.VMEM((len(flips), tokens, width), grads.dtype),
            pltpu.VMEM((len(flips), *basis_in.shape[1:]), basis_in.dtype),
            pltpu.VMEM((len(flips), *basis_out.shape[1:]), basis_out.dtype),
            pltpu.VMEM((tokens // 16, both), jnp.float32),
            pltpu.SemaphoreType.DMA((2, steps)),
            pltpu.SemaphoreType.DMA((3, len(flips))),
        ],
        compiler_params=pltpu.CompilerParams(vmem_limit_bytes=VMEM),
    )(*(pltpu.with_memory_space_constraint(x, pltpu.HBM) for x in operands), *inside)


def decode(ref, tokens):
    shared = ref.shape[0] - tokens
    both = ref.shape[1]
    log = ref[pl.ds(tokens, shared), :].astype(jnp.int32).astype(jnp.float32)
    scale = jnp.exp2(log * (1.0 / STEPS)) * (1.0 / TOP)
    codes = ref[pl.ds(0, tokens), :].astype(jnp.int32).astype(jnp.float32)
    return (codes.reshape(shared, tokens // shared, both) * scale[:, None, :]).reshape(tokens, both)


def add_up(total, partial, out):
    out[...] = total[...] + decode(partial, total.shape[0])


def weigh(lengths, weights):
    tokens, both = weights.shape
    count = lengths[lax.axis_index("tensor") % lengths.shape[0]]
    row = lax.broadcasted_iota(jnp.int32, (tokens, both), 0)
    lane = lax.broadcasted_iota(jnp.int32, (1, both), 1)
    share = 1.0 / jnp.full((1, both), count, jnp.int32).astype(jnp.float32)
    weights[...] = jnp.where(row < count, jnp.where(lane < both // 2, share, 1.0), 0.0)


def outer(weights, most, last, out, grad):
    tokens, both = most.shape
    half = both // 2
    weighted = (most[...] + decode(last, tokens)) * weights[...]
    first = weighted.astype(jnp.bfloat16)
    rest = (weighted - first.astype(jnp.float32)).astype(jnp.bfloat16)
    wide = tn(first, jnp.concatenate([first, rest], axis=1))
    product = wide[:, :both] + (wide[:, both:] + tn(rest, first))
    grad[...] = product[:half, :]
    even = grad[pl.ds(0, half // 2, stride=2), :][:, half:]
    odd = grad[pl.ds(1, half // 2, stride=2), :][:, half:]
    blocks = jnp.concatenate([even, odd], axis=1)
    block_rows = blocks.shape[0] // 2
    for t in range(4):
        for x in range(2):
            out[t * 2 + x] = blocks[x * block_rows : (x + 1) * block_rows]


def through_fisher(grads, fisher, beside, out):
    layers, _, width = fisher.shape
    lanes = grads.shape[2]
    rows = grads.shape[0] // layers
    depth = grads.shape[1] * lanes // 2
    core = lax.axis_index("core")
    steps = depth // lanes
    order = [e * 2 + x for x in range(2) for e in range(rows // 2)]
    every = []
    for layer in range(layers):
        mapped = None
        for block, owner in ((fisher, core), (beside, 1 - core)):
            parts = [
                jnp.concatenate([grads[layer * rows + s, pl.ds(owner * steps + r, 1), :] for s in order], axis=0)
                for r in range(steps)
            ]
            term = nn(thirds(jnp.concatenate(parts, axis=1)), block[layer, pl.ds(0, depth), :])
            mapped = term if mapped is None else mapped + term
        every.append(add_thirds(mapped))
    for x in range(2):
        own = jnp.concatenate([mapped[x * rows // 2 : (x + 1) * rows // 2] for mapped in every], axis=0)
        pieces = [own[:, at : at + lanes] for at in range(0, width, lanes)]
        most = jnp.abs(pieces[0])
        for piece in pieces[1:]:
            most = jnp.maximum(most, jnp.abs(piece))
        log = jnp.ceil(jnp.log2(jnp.maximum(most, 1e-30)) * STEPS)
        scale = jnp.exp2(log * (-1.0 / STEPS)) * TOP
        pieces = [jnp.minimum(jnp.maximum(jnp.round(piece * scale), -TOP), TOP) for piece in pieces] + [log]
        rest = out.shape[1] - own.shape[0] * len(pieces)
        message = jnp.concatenate([*pieces, jnp.zeros((rest, lanes), jnp.float32)], axis=0)
        message = message.astype(jnp.int32).astype(jnp.int16)
        for t in range(4):
            out[t * 2 + x] = message


def with_queries(mapped, own, beside, across, corner, out):
    layers, depth, count = own.shape
    lanes = mapped.shape[2]
    examples = out.shape[0]
    rows = layers * examples
    here = lax.axis_index("x") * 2 + lax.axis_index("core")

    def read(source):
        message = mapped[source].astype(jnp.int32).astype(jnp.float32)
        last = depth // lanes * rows
        scale = jnp.exp2(message[last : last + rows] * (1.0 / STEPS)) * (1.0 / TOP)
        return jnp.concatenate([message[at : at + rows] * scale for at in range(0, last, rows)], axis=1)

    sums = [None] * layers
    for k, block in enumerate((own, beside, across, corner)):
        left = thirds(read((here ^ k) * 2) + read((here ^ k) * 2 + 1))
        for layer in range(layers):
            term = nn(left, block[layer]) if k < 2 else nt(left, block[layer])
            sums[layer] = term if sums[layer] is None else sums[layer] + term
    result = None
    for layer in range(layers):
        scores = add_thirds(sums[layer])[layer * examples : (layer + 1) * examples]
        result = scores if result is None else result + scores
    out[...] = result


def swap(x, axis, flip):
    return lax.ppermute(x, axis, [(i, i ^ flip) for i in range(lax.axis_size(axis))])


def in_vmem(x):
    return pltpu.with_memory_space_constraint(x, pltpu.VMEM)


def small(acts_in, grads_out, basis_in, basis_out, lengths, fisher_inv, queries):
    vmem = pl.BlockSpec(memory_space=pltpu.VMEM)
    params = pltpu.CompilerParams(vmem_limit_bytes=VMEM)
    proj_width = basis_in.shape[2]
    operands = (acts_in, grads_out, jnp.swapaxes(basis_in, 1, 2), jnp.swapaxes(basis_out, 1, 2))

    across, beside = swap(queries, "x", 1), swap(queries, "core", 1)
    (far,) = projector((3,), (32,), PIECES_ONE, *operands)
    acts_in, grads_out, far = lax.optimization_barrier((acts_in, grads_out, far))
    middle, near = projector((2, 1), (32, 32), PIECES_TWO, acts_in, grads_out, *operands[2:])
    acts_in, middle, near = lax.optimization_barrier((acts_in, middle, near))
    queries, beside, weights, here = projector(
        (0,), (0,), PIECES_ONE, acts_in, grads_out, *operands[2:], queries, beside, lengths
    )
    far, middle = swap(far, "tensor", 3), swap(middle, "tensor", 2)
    near = swap(near, "tensor", 1)
    fisher_beside = swap(fisher_inv, "core", 1)

    for partial in (far, middle):
        here = pl.pallas_call(
            add_up,
            out_shape=jax.ShapeDtypeStruct(here.shape, jnp.float32),
            in_specs=[vmem] * 2,
            out_specs=vmem,
            compiler_params=params,
        )(here, partial)

    blocks = pl.pallas_call(
        outer,
        out_shape=jax.ShapeDtypeStruct((8, proj_width // 4, 2 * proj_width), jnp.float32),
        in_specs=[vmem] * 3,
        out_specs=vmem,
        scratch_shapes=[pltpu.VMEM((proj_width, 2 * proj_width), jnp.float32)],
        compiler_params=params,
    )(weights, here, near)
    blocks, fisher_beside = lax.optimization_barrier((blocks, fisher_beside))
    blocks = lax.all_to_all(blocks, ("tensor", "x"), 0, 0, tiled=True)

    mapped = pl.pallas_call(
        through_fisher,
        out_shape=jax.ShapeDtypeStruct((8, 48, 128), jnp.int16),
        in_specs=[vmem] * 3,
        out_specs=vmem,
        compiler_params=params,
    )(blocks, in_vmem(fisher_inv), in_vmem(fisher_beside))
    across, mapped = lax.optimization_barrier((across, mapped))
    corner = swap(across, "core", 1)
    mapped = lax.all_to_all(mapped, ("tensor", "x"), 0, 0, tiled=True)

    return pl.pallas_call(
        with_queries,
        out_shape=jax.ShapeDtypeStruct((acts_in.shape[1], queries.shape[2]), jnp.float32),
        in_specs=[vmem] * 5,
        out_specs=vmem,
        compiler_params=params,
    )(mapped, queries, beside, across, corner)


def general(acts_in, grads_out, basis_in, basis_out, lengths, fisher_inv, queries):
    proj_width = basis_in.shape[2]
    layer_count = acts_in.shape[0]
    local_examples = acts_in.shape[1]
    proj_in = jnp.einsum("letd,ldr->letr", acts_in, basis_in, preferred_element_type=jnp.float32)
    proj_out = jnp.einsum(
        "letd,ldr->letr", grads_out, basis_out, preferred_element_type=jnp.float32
    )
    partial_proj = jnp.concatenate([proj_out, proj_in], axis=3)
    summed_proj = lax.psum(partial_proj, "tensor")
    share_len = summed_proj.shape[2]
    proj_out = summed_proj[..., :proj_width]
    proj_in = summed_proj[..., proj_width:]
    positions = lax.broadcasted_iota(jnp.int32, (share_len,), 0)
    token_weight = jnp.where(positions[None, :] < lengths[:, None], 1.0, 0.0).astype(jnp.float32)
    token_weight = token_weight / lengths[:, None].astype(jnp.float32)
    weighted = proj_out * token_weight[None, :, :, None]
    outer_prod = jnp.einsum("leta,letb->leab", weighted, proj_in, precision=lax.Precision.HIGHEST)
    example_grads = outer_prod.reshape(layer_count, local_examples, proj_width * proj_width)
    row_blocks = lax.all_to_all(example_grads, "dp", split_axis=2, concat_axis=1, tiled=True)
    gathered_queries = lax.all_gather(queries, "dp", axis=2, tiled=True)
    mapped = jnp.einsum(
        "lqj,lij->lqi",
        gathered_queries,
        lax.all_gather(fisher_inv, "tensor", axis=2, tiled=True),
        preferred_element_type=jnp.float32,
    )
    score_terms = jnp.einsum("lei,lqi->eq", row_blocks, mapped, precision=lax.Precision.HIGHEST)
    return lax.psum_scatter(score_terms, "dp", scatter_dimension=0, tiled=True)


def solution(mesh):
    dp = ("dp",)
    local = general
    if (mesh.shape["parts"], mesh.shape["tensor"], mesh.shape["dp"]) == (2, 4, 4):
        mesh = jax.sharding.Mesh(mesh.devices.reshape(2, 4, 2, 2), ("parts", "tensor", "x", "core"))
        dp = ("x", "core")
        local = small
    in_specs = (
        P(None, ("parts", *dp), None, "tensor"),
        P(None, ("parts", *dp), None, "tensor"),
        P(None, "tensor", None),
        P(None, "tensor", None),
        P(("parts", *dp)),
        P(None, dp, "tensor"),
        P(None, "tensor", dp),
    )
    out_specs = P(("parts", *dp), "tensor")
    return jax.shard_map(local, mesh=mesh, in_specs=in_specs, out_specs=out_specs, check_vma=False)
```

```python
import jax
import jax.numpy as jnp
from jax import lax
from jax.experimental import pallas as pl
from jax.experimental.pallas import tpu as pltpu
from jax.sharding import PartitionSpec as P

STEPS = 64.0
TOP = 32767.0
PIECES_TWO = ((128, 384), (256, 256))
PIECES_ONE = ((128, 384),)
AHEAD = 2
VMEM = 24 * 1024 * 1024


def nn(a, b):
    return lax.dot_general(a, b, (((1,), (0,)), ((), ())), preferred_element_type=jnp.float32)


def nt(a, b):
    return lax.dot_general(a, b, (((1,), (1,)), ((), ())), preferred_element_type=jnp.float32)


def tn(a, b):
    return lax.dot_general(a, b, (((0,), (0,)), ((), ())), preferred_element_type=jnp.float32)


def thirds(x):
    first = x.astype(jnp.bfloat16).astype(jnp.float32)
    rest = x - first
    second = rest.astype(jnp.bfloat16).astype(jnp.float32)
    return jnp.concatenate([first, second, rest - second], axis=0).astype(jnp.bfloat16)


def add_thirds(x):
    rows = x.shape[0] // 3
    return x[:rows] + (x[rows : 2 * rows] + x[2 * rows :])


def project(flips, groups, pieces, turn, acts, grads, basis_in, basis_out, *refs):
    *refs, a_buf, g_buf, in_buf, out_buf, scale_log, sems, basis_sems = refs
    queries = beside = lengths = turned = turned_beside = weights = turn_buf = None
    if turn:
        *refs, turn_buf = refs
        queries, beside, lengths, turned, turned_beside, weights, *refs = refs
    outs = refs
    examples, tokens = acts.shape[1], acts.shape[2]
    here = lax.axis_index("tensor")
    layers = [(here ^ flip) // examples for flip in flips]
    first = []
    for k, layer in enumerate(layers):
        first.append(pltpu.make_async_copy(basis_out.at[layer], out_buf.at[k], basis_sems.at[0, k]))
        first.append(pltpu.make_async_copy(basis_in.at[layer], in_buf.at[k], basis_sems.at[1, k]))
    if turn:
        first.append(pltpu.make_async_copy(queries, turn_buf, basis_sems.at[2, 0]))
    copies, spans = [], []
    for k, flip in enumerate(flips):
        example = (here ^ flip) % examples
        begin = 0
        for size in pieces[k]:
            rows, at = pl.ds(begin, size), len(copies)
            spans.append((k, begin, size))
            copies.append(
                (
                    pltpu.make_async_copy(grads.at[layers[k], example, rows, :], g_buf.at[k, rows, :], sems.at[0, at]),
                    pltpu.make_async_copy(acts.at[layers[k], example, rows, :], a_buf.at[k, rows, :], sems.at[1, at]),
                )
            )
            begin += size
    for copy in first:
        copy.start()
    for c in range(AHEAD):
        for copy in copies[c]:
            copy.start()
    for copy in first:
        copy.wait()
    if turn:
        for i in range(turned.shape[0]):
            turned[i] = turn_buf[i].T
            turned_beside[i] = beside[i].T
        weigh(lengths, weights)
    for at, (k, begin, size) in enumerate(spans):
        group, out, rows = groups[k], outs[k], pl.ds(begin, size)
        for copy in copies[at]:
            copy.wait()
        if at + AHEAD < len(copies):
            for copy in copies[at + AHEAD]:
                copy.start()
        proj_out = nt(g_buf[k, rows, :], out_buf[k])
        proj_in = nt(a_buf[k, rows, :], in_buf[k])
        both = jnp.concatenate([proj_out, proj_in], axis=1)
        if not group:
            out[rows, :] = both
            continue
        grouped = both.reshape(size // group, group, both.shape[1])
        most = jnp.maximum(jnp.max(jnp.abs(grouped), axis=1), 1e-30)
        log = jnp.ceil(jnp.log2(most) * STEPS)
        scale = jnp.exp2(log * (-1.0 / STEPS)) * TOP
        codes = jnp.round(grouped * scale[:, None, :])
        codes = jnp.minimum(jnp.maximum(codes, -TOP), TOP).reshape(both.shape)
        out[rows, :] = codes.astype(jnp.int32).astype(jnp.int16)
        scale_log[pl.ds(begin // group, size // group), :] = log
        if begin + size == tokens:
            log = scale_log[pl.ds(0, tokens // group), :]
            out[pl.ds(tokens, tokens // group), :] = log.astype(jnp.int32).astype(jnp.int16)


def projector(flips, groups, pieces, acts, grads, basis_in, basis_out, queries=None, beside=None, lengths=None):
    tokens, width = acts.shape[2], acts.shape[3]
    both = 2 * basis_in.shape[1]
    steps = sum(len(p) for p in pieces)
    operands, inside, turned, turn_buf = [acts, grads, basis_in, basis_out], [], [], []
    if queries is not None:
        operands.append(queries)
        inside += [beside, lengths]
        layers, count, depth = queries.shape
        turned = [jax.ShapeDtypeStruct((layers, depth, count), queries.dtype)] * 2
        turned.append(jax.ShapeDtypeStruct((tokens, both), jnp.float32))
        turn_buf = [pltpu.VMEM(queries.shape, queries.dtype)]
    hbm = pl.BlockSpec(memory_space=pltpu.HBM)
    vmem, smem = pl.BlockSpec(memory_space=pltpu.VMEM), pl.BlockSpec(memory_space=pltpu.SMEM)

    def project_pairs(*refs):
        project(flips, groups, pieces, queries is not None, *refs)

    return pl.pallas_call(
        project_pairs,
        out_shape=turned
        + [
            jax.ShapeDtypeStruct((tokens + tokens // g, both), jnp.int16)
            if g
            else jax.ShapeDtypeStruct((tokens, both), jnp.float32)
            for g in groups
        ],
        in_specs=[hbm] * len(operands) + [vmem, smem][: len(inside)],
        out_specs=[vmem] * (len(turned) + len(groups)),
        scratch_shapes=turn_buf
        + [
            pltpu.VMEM((len(flips), tokens, width), acts.dtype),
            pltpu.VMEM((len(flips), tokens, width), grads.dtype),
            pltpu.VMEM((len(flips), *basis_in.shape[1:]), basis_in.dtype),
            pltpu.VMEM((len(flips), *basis_out.shape[1:]), basis_out.dtype),
            pltpu.VMEM((tokens // 16, both), jnp.float32),
            pltpu.SemaphoreType.DMA((2, steps)),
            pltpu.SemaphoreType.DMA((3, len(flips))),
        ],
        compiler_params=pltpu.CompilerParams(vmem_limit_bytes=VMEM),
    )(*(pltpu.with_memory_space_constraint(x, pltpu.HBM) for x in operands), *inside)


def decode(ref, tokens):
    shared = ref.shape[0] - tokens
    both = ref.shape[1]
    log = ref[pl.ds(tokens, shared), :].astype(jnp.int32).astype(jnp.float32)
    scale = jnp.exp2(log * (1.0 / STEPS)) * (1.0 / TOP)
    codes = ref[pl.ds(0, tokens), :].astype(jnp.int32).astype(jnp.float32)
    return (codes.reshape(shared, tokens // shared, both) * scale[:, None, :]).reshape(tokens, both)


def add_up(total, partial, out):
    out[...] = total[...] + decode(partial, total.shape[0])


def weigh(lengths, weights):
    tokens, both = weights.shape
    count = lengths[lax.axis_index("tensor") % lengths.shape[0]]
    row = lax.broadcasted_iota(jnp.int32, (tokens, both), 0)
    lane = lax.broadcasted_iota(jnp.int32, (1, both), 1)
    share = 1.0 / jnp.full((1, both), count, jnp.int32).astype(jnp.float32)
    weights[...] = jnp.where(row < count, jnp.where(lane < both // 2, share, 1.0), 0.0)


def outer(weights, most, last, out, grad):
    tokens, both = most.shape
    half = both // 2
    weighted = (most[...] + decode(last, tokens)) * weights[...]
    first = weighted.astype(jnp.bfloat16)
    rest = (weighted - first.astype(jnp.float32)).astype(jnp.bfloat16)
    wide = tn(first, jnp.concatenate([first, rest], axis=1))
    product = wide[:, :both] + (wide[:, both:] + tn(rest, first))
    grad[...] = product[:half, :]
    even = grad[pl.ds(0, half // 2, stride=2), :][:, half:]
    odd = grad[pl.ds(1, half // 2, stride=2), :][:, half:]
    blocks = jnp.concatenate([even, odd], axis=1)
    block_rows = blocks.shape[0] // 2
    for t in range(4):
        for x in range(2):
            out[t * 2 + x] = blocks[x * block_rows : (x + 1) * block_rows]


def through_fisher(grads, fisher, beside, out):
    layers, _, width = fisher.shape
    lanes = grads.shape[2]
    rows = grads.shape[0] // layers
    depth = grads.shape[1] * lanes // 2
    core = lax.axis_index("core")
    steps = depth // lanes
    order = [e * 2 + x for x in range(2) for e in range(rows // 2)]
    every = []
    for layer in range(layers):
        mapped = None
        for block, owner in ((fisher, core), (beside, 1 - core)):
            parts = [
                jnp.concatenate([grads[layer * rows + s, pl.ds(owner * steps + r, 1), :] for s in order], axis=0)
                for r in range(steps)
            ]
            term = nn(thirds(jnp.concatenate(parts, axis=1)), block[layer, pl.ds(0, depth), :])
            mapped = term if mapped is None else mapped + term
        every.append(add_thirds(mapped))
    for x in range(2):
        own = jnp.concatenate([mapped[x * rows // 2 : (x + 1) * rows // 2] for mapped in every], axis=0)
        pieces = [own[:, at : at + lanes] for at in range(0, width, lanes)]
        most = jnp.abs(pieces[0])
        for piece in pieces[1:]:
            most = jnp.maximum(most, jnp.abs(piece))
        log = jnp.ceil(jnp.log2(jnp.maximum(most, 1e-30)) * STEPS)
        scale = jnp.exp2(log * (-1.0 / STEPS)) * TOP
        pieces = [jnp.minimum(jnp.maximum(jnp.round(piece * scale), -TOP), TOP) for piece in pieces] + [log]
        rest = out.shape[1] - own.shape[0] * len(pieces)
        message = jnp.concatenate([*pieces, jnp.zeros((rest, lanes), jnp.float32)], axis=0)
        message = message.astype(jnp.int32).astype(jnp.int16)
        for t in range(4):
            out[t * 2 + x] = message


def with_queries(mapped, own, beside, across, corner, out):
    layers, depth, count = own.shape
    lanes = mapped.shape[2]
    examples = out.shape[0]
    rows = layers * examples
    here = lax.axis_index("x") * 2 + lax.axis_index("core")

    def read(source):
        message = mapped[source].astype(jnp.int32).astype(jnp.float32)
        last = depth // lanes * rows
        scale = jnp.exp2(message[last : last + rows] * (1.0 / STEPS)) * (1.0 / TOP)
        return jnp.concatenate([message[at : at + rows] * scale for at in range(0, last, rows)], axis=1)

    sums = None
    for k, block in enumerate((own, beside, across, corner)):
        left = thirds(read((here ^ k) * 2) + read((here ^ k) * 2 + 1))
        for layer in range(layers):
            wanted = jnp.concatenate([left[at + layer * examples : at + (layer + 1) * examples] for at in range(0, 3 * rows, rows)], axis=0)
            term = nn(wanted, block[layer]) if k < 2 else nt(wanted, block[layer])
            sums = term if sums is None else sums + term
    out[...] = add_thirds(sums)


def swap(x, axis, flip):
    return lax.ppermute(x, axis, [(i, i ^ flip) for i in range(lax.axis_size(axis))])


def in_vmem(x):
    return pltpu.with_memory_space_constraint(x, pltpu.VMEM)


def small(acts_in, grads_out, basis_in, basis_out, lengths, fisher_inv, queries):
    vmem = pl.BlockSpec(memory_space=pltpu.VMEM)
    params = pltpu.CompilerParams(vmem_limit_bytes=VMEM)
    proj_width = basis_in.shape[2]
    operands = (acts_in, grads_out, jnp.swapaxes(basis_in, 1, 2), jnp.swapaxes(basis_out, 1, 2))

    beside, across = swap(queries, "core", 1), swap(queries, "x", 1)
    (far,) = projector((3,), (32,), PIECES_ONE, *operands)
    acts_in, grads_out, far = lax.optimization_barrier((acts_in, grads_out, far))
    middle, near = projector((2, 1), (32, 32), PIECES_TWO, acts_in, grads_out, *operands[2:])
    acts_in, middle, near = lax.optimization_barrier((acts_in, middle, near))
    queries, beside, weights, here = projector(
        (0,), (0,), PIECES_ONE, acts_in, grads_out, *operands[2:], queries, beside, lengths
    )
    far, middle = swap(far, "tensor", 3), swap(middle, "tensor", 2)
    near = swap(near, "tensor", 1)
    fisher_beside = swap(fisher_inv, "core", 1)

    for partial in (far, middle):
        here = pl.pallas_call(
            add_up,
            out_shape=jax.ShapeDtypeStruct(here.shape, jnp.float32),
            in_specs=[vmem] * 2,
            out_specs=vmem,
            compiler_params=params,
        )(here, partial)

    blocks = pl.pallas_call(
        outer,
        out_shape=jax.ShapeDtypeStruct((8, proj_width // 4, 2 * proj_width), jnp.float32),
        in_specs=[vmem] * 3,
        out_specs=vmem,
        scratch_shapes=[pltpu.VMEM((proj_width, 2 * proj_width), jnp.float32)],
        compiler_params=params,
    )(weights, here, near)
    blocks, fisher_beside = lax.optimization_barrier((blocks, fisher_beside))
    blocks = lax.all_to_all(blocks, ("tensor", "x"), 0, 0, tiled=True)

    mapped = pl.pallas_call(
        through_fisher,
        out_shape=jax.ShapeDtypeStruct((8, 48, 128), jnp.int16),
        in_specs=[vmem] * 3,
        out_specs=vmem,
        compiler_params=params,
    )(blocks, in_vmem(fisher_inv), in_vmem(fisher_beside))
    across, mapped = lax.optimization_barrier((across, mapped))
    corner = swap(across, "core", 1)
    mapped = lax.all_to_all(mapped, ("tensor", "x"), 0, 0, tiled=True)

    return pl.pallas_call(
        with_queries,
        out_shape=jax.ShapeDtypeStruct((acts_in.shape[1], queries.shape[2]), jnp.float32),
        in_specs=[vmem] * 5,
        out_specs=vmem,
        compiler_params=params,
    )(mapped, queries, beside, across, corner)


def general(acts_in, grads_out, basis_in, basis_out, lengths, fisher_inv, queries):
    proj_width = basis_in.shape[2]
    layer_count = acts_in.shape[0]
    local_examples = acts_in.shape[1]
    proj_in = jnp.einsum("letd,ldr->letr", acts_in, basis_in, preferred_element_type=jnp.float32)
    proj_out = jnp.einsum(
        "letd,ldr->letr", grads_out, basis_out, preferred_element_type=jnp.float32
    )
    partial_proj = jnp.concatenate([proj_out, proj_in], axis=3)
    summed_proj = lax.psum(partial_proj, "tensor")
    share_len = summed_proj.shape[2]
    proj_out = summed_proj[..., :proj_width]
    proj_in = summed_proj[..., proj_width:]
    positions = lax.broadcasted_iota(jnp.int32, (share_len,), 0)
    token_weight = jnp.where(positions[None, :] < lengths[:, None], 1.0, 0.0).astype(jnp.float32)
    token_weight = token_weight / lengths[:, None].astype(jnp.float32)
    weighted = proj_out * token_weight[None, :, :, None]
    outer_prod = jnp.einsum("leta,letb->leab", weighted, proj_in, precision=lax.Precision.HIGHEST)
    example_grads = outer_prod.reshape(layer_count, local_examples, proj_width * proj_width)
    row_blocks = lax.all_to_all(example_grads, "dp", split_axis=2, concat_axis=1, tiled=True)
    gathered_queries = lax.all_gather(queries, "dp", axis=2, tiled=True)
    mapped = jnp.einsum(
        "lqj,lij->lqi",
        gathered_queries,
        lax.all_gather(fisher_inv, "tensor", axis=2, tiled=True),
        preferred_element_type=jnp.float32,
    )
    score_terms = jnp.einsum("lei,lqi->eq", row_blocks, mapped, precision=lax.Precision.HIGHEST)
    return lax.psum_scatter(score_terms, "dp", scatter_dimension=0, tiled=True)


def solution(mesh):
    dp = ("dp",)
    local = general
    if (mesh.shape["parts"], mesh.shape["tensor"], mesh.shape["dp"]) == (2, 4, 4):
        mesh = jax.sharding.Mesh(mesh.devices.reshape(2, 4, 2, 2), ("parts", "tensor", "x", "core"))
        dp = ("x", "core")
        local = small
    in_specs = (
        P(None, ("parts", *dp), None, "tensor"),
        P(None, ("parts", *dp), None, "tensor"),
        P(None, "tensor", None),
        P(None, "tensor", None),
        P(("parts", *dp)),
        P(None, dp, "tensor"),
        P(None, "tensor", dp),
    )
    out_specs = P(("parts", *dp), "tensor")
    return jax.shard_map(local, mesh=mesh, in_specs=in_specs, out_specs=out_specs, check_vma=False)
```
